32 devices in a mesh: dom: 16 (over z, y, core), grid: 2 (over x).
Axes of the slice: x: 2, y: 2, z: 4, core: 2. Of those that a mesh axis runs over, the one named last changes fastest.
Arguments:
- rhs: bfloat16 [2, 96, 16, 320], P('grid', 'dom'), may hold values from -24 to 24
- blocks: bfloat16 [2, 96, 3, 320, 320], P('grid', 'dom'), may hold values from -0.1875 to 0.1875
- offsets: int32 [2, 96, 3], P('grid', 'dom'), may hold values from -1 to 1
- donor_elem: int32 [2, 16, 2, 2], P('grid', 'dom'), may hold values from 0 to 5
- fringe_elem: int32 [2, 16, 2, 2], P('grid', 'dom'), may hold values from 0 to 5
- donor_weight: float32 [2, 16, 2, 2], P('grid', 'dom'), may hold values from 0.25 to 1
- fringe_count: int32 [2, 16, 2], P('grid', 'dom'), may hold values from 0 to 2, as said below
Outputs:
- powers: bfloat16 [2, 96, 4, 16, 320], P('grid', 'dom')
- r_factor: float32 [80, 80], replicated
The draws below stay inside these ranges and needn't reach their ends.
Inputs may be any that keep to these rules, and one draw needn't show every extreme that they name: `fringe_count`: the count from a grid to its own partitions is 0. In every draw some partition of each grid receives 2 slots from every other grid.
All inputs are finite; a program needn't handle non-finite values.
Results may differ from the reference program's by a relative error of at most 0.0033.
The reference program's roundings to bfloat16 on the way count: a program that leaves them out, or rounds other values in their place, can miss the bound.
Values may be sent and summed in bfloat16 or wider, within the bound.
No kernel may reach another device: no remote copies, remote signals or barrier semaphores. Data moves between devices by JAX's collectives and lax.ppermute only.
A program may use at most 64 MiB of HBM per device.

```python
import jax
import jax.numpy as jnp
from jax import lax

W = 320
R = 16
S = 4
NB = 3
H = 1
C = 2
E = 6
GRIDS = 2
PARTS_SIZE = 16
ELEMS = 96
COLS = 80


def draw_rhs(key, part):
    position = jnp.arange(ELEMS, dtype=jnp.float32) / max(ELEMS - 1, 1)
    rising = 1.0 + 2.0 * position
    grid_rise = 1.0 + jnp.arange(GRIDS, dtype=jnp.float32) / max(GRIDS - 1, 1)
    profile = grid_rise[:, None, None, None] * rising[None, :, None, None]
    values = jnp.clip(jax.random.normal(key, (GRIDS, ELEMS, R, W), jnp.float32), -4.0, 4.0)
    return jnp.clip(values * profile, -24.0, 24.0).astype(jnp.bfloat16)


def draw_fringe_count(key, part):
    counts = jax.random.randint(key, (GRIDS, PARTS_SIZE, GRIDS), 0, C + 1)
    full_part = jax.random.randint(jax.random.fold_in(key, 7), (GRIDS,), 0, PARTS_SIZE)
    part_ids = jnp.arange(PARTS_SIZE, dtype=jnp.int32)[None, :, None]
    counts = jnp.where(part_ids == full_part[:, None, None], C, counts)
    same_grid = jnp.arange(GRIDS, dtype=jnp.int32)[:, None, None] == jnp.arange(GRIDS, dtype=jnp.int32)[None, None, :]
    return jnp.where(same_grid, 0, counts).astype(jnp.int32)


def with_ends(result, rng, least, top_value):
    spot = [jax.random.randint(jax.random.fold_in(rng, axis), (), 0, length) for axis, length in enumerate(result.shape)]
    widest = result.shape.index(max(result.shape))
    neighbour = spot[:widest] + [(spot[widest] + 1) % result.shape[widest]] + spot[widest + 1:]
    return result.at[tuple(spot)].set(least).at[tuple(neighbour)].set(top_value)


def levels(rng, extent, split, low, top_value):
    gain = 1.0
    for dim, shards_of in split:
        draws = jax.random.uniform(jax.random.fold_in(jax.random.fold_in(rng, 6), dim), (shards_of,), jnp.float32, low / len(split), top_value / len(split))
        gain = gain * jnp.repeat(jnp.exp(draws), extent[dim] // shards_of).reshape((-1,) + (1,) * (len(extent) - 1 - dim))
    return gain


def normal_values(own_key, dims, width, most, split=(), held_as=jnp.bfloat16):
    level = levels(own_key, dims, split, -0.22, 0.18) if split else 1.0
    entries = jax.random.normal(own_key, dims, jnp.float32) * width * level
    return jnp.minimum(jnp.maximum(entries, -most), most).astype(held_as)


def setup_inputs(seed: int = 0) -> dict:
    arg_keys = jax.random.split(jax.random.key(seed), 8)
    return {
        "rhs": draw_rhs(jax.random.fold_in(arg_keys[7], 71), 0),
        "blocks": normal_values(arg_keys[1], (GRIDS, ELEMS, NB, W, W), (NB * W) ** -0.5, 0.1875, ((0, 2), (1, 16))),
        "offsets": with_ends(jax.random.randint(arg_keys[2], (GRIDS, ELEMS, NB), 0 - H, H + 1), jax.random.fold_in(arg_keys[2], 1), 0 - H, H).astype(jnp.int32),
        "donor_elem": with_ends(jax.random.randint(arg_keys[3], (GRIDS, PARTS_SIZE, GRIDS, C), 0, E), jax.random.fold_in(arg_keys[3], 1), 0, E - 1).astype(jnp.int32),
        "fringe_elem": with_ends(jax.random.randint(arg_keys[4], (GRIDS, PARTS_SIZE, GRIDS, C), 0, E), jax.random.fold_in(arg_keys[4], 1), 0, E - 1).astype(jnp.int32),
        "donor_weight": jnp.clip(0.25 + 0.75 * jax.random.uniform(arg_keys[5], (GRIDS, PARTS_SIZE, GRIDS, C), jnp.float32) ** levels(arg_keys[5], (GRIDS, PARTS_SIZE, GRIDS, C), ((0, 2), (1, 16)), -0.2, 0.2), 0.25, 1.0),
        "fringe_count": draw_fringe_count(jax.random.fold_in(arg_keys[7], 71), 0),
    }


def one_part(pair):
    return jnp.einsum('ekra,ekab->erb', pair[0].astype(jnp.float32), pair[1].astype(jnp.float32))

def apply_operator(field, blocks, offsets, donor_elem, fringe_elem, donor_weight, fringe_count):
    padded = jnp.pad(field, ((0, 0), (H, H), (0, 0), (0, 0)))
    col_index = jnp.arange(ELEMS, dtype=jnp.int32)[None, :, None] + offsets + H
    taken_cols = jax.vmap(lambda plane, where_from: plane[where_from])(padded, col_index)
    pieces = taken_cols.reshape(GRIDS * PARTS_SIZE, E, NB, R, W)
    block_rows = blocks.reshape(GRIDS * PARTS_SIZE, E, NB, W, W)
    blockpart = lax.map(one_part, (pieces, block_rows)).reshape(GRIDS, ELEMS, R, W)
    flat_field = field.reshape(GRIDS * ELEMS, R, W)
    source_index = jnp.arange(GRIDS, dtype=jnp.int32)[None, None, :, None] * ELEMS + jnp.arange(PARTS_SIZE, dtype=jnp.int32)[None, :, None, None] * E + donor_elem
    picked = flat_field[source_index]
    live_slot = jnp.arange(C, dtype=jnp.int32)[None, None, None, :] < fringe_count[..., None]
    weights = jnp.where(live_slot, donor_weight, jnp.zeros_like(donor_weight))
    hit_target = fringe_elem[..., None] == jnp.arange(E, dtype=jnp.int32)
    spread = jnp.where(hit_target, weights[..., None], jnp.zeros_like(weights[..., None]))
    donorpart = jnp.einsum('hpgce,hpgcrw->hperw', spread, picked.astype(jnp.float32), precision=lax.Precision.HIGHEST).reshape(GRIDS, ELEMS, R, W)
    return (blockpart + donorpart).astype(jnp.bfloat16)

def reference(rhs, blocks, offsets, donor_elem, fringe_elem, donor_weight, fringe_count):
    basis = [rhs]
    field = rhs
    for level in range(S):
        field = apply_operator(field, blocks, offsets, donor_elem, fringe_elem, donor_weight, fringe_count)
        basis.append(field)
    stacked = jnp.stack(basis, axis=2).astype(jnp.float32)
    gram = jnp.einsum('gnkrw,gnlqw->krlq', stacked, stacked, precision=lax.Precision.HIGHEST)
    gram = gram.reshape(COLS, COLS) / (GRIDS * ELEMS * W)
    r_factor = jnp.linalg.cholesky(gram).T
    powers = jnp.stack(basis[1:], axis=2)
    return (powers, r_factor)
```

```python
import functools

import jax
import jax.numpy as jnp
from jax import lax
from jax.experimental import pallas as pl
from jax.experimental.pallas import tpu as pltpu
from jax.sharding import Mesh
from jax.sharding import PartitionSpec as P

S = 4
H = 1
CORES = 2

VMEM = pl.BlockSpec(memory_space=pltpu.VMEM)
SMEM = pl.BlockSpec(memory_space=pltpu.SMEM)


def edges_kernel(v_ref, side_ref, chip_ref):
    last = v_ref.shape[0] - 1
    core = lax.axis_index("core")
    side_ref[...] = v_ref[core * last]
    chip_ref[...] = v_ref[(1 - core) * last]


def inner_kernel(offsets_ref, v_ref, blocks_ref, acc_ref):
    count, kinds = blocks_ref.shape[:2]
    for e in range(count):
        total = None
        for k in range(kinds):
            col = e + offsets_ref[0, e, k]
            inside = jnp.logical_and(col >= 0, col < count)
            lhs = v_ref[jnp.clip(col, 0, count - 1)]
            lhs = jnp.where(inside, lhs, jnp.zeros_like(lhs))
            part = jnp.dot(lhs, blocks_ref[e, k], preferred_element_type=jnp.float32)
            total = part if total is None else total + part
        acc_ref[e] = total


def outer_kernel(
    grids, offsets_ref, donor_ref, fringe_ref, weight_ref, live_ref,
    acc_ref, blocks_ref, side_ref, chip_ref, *rest
):
    others, (v_ref, side_out, chip_out, total_ref) = rest[: grids - 1], rest[grids - 1 :]
    count, kinds = blocks_ref.shape[:2]
    last = count - 1
    chips = lax.axis_size("chip")
    chip, core, grid = (lax.axis_index(a) for a in ("chip", "core", "grid"))
    total_ref[...] = acc_ref[...]
    has_before = jnp.logical_or(chip > 0, core > 0)
    has_after = jnp.logical_or(chip < chips - 1, core == 0)
    before = jnp.where(core == 0, side_ref[...], chip_ref[...])
    after = jnp.where(core == 0, chip_ref[...], side_ref[...])
    for e, halo, there, offset in ((0, before, has_before, -H), (last, after, has_after, H)):
        for k in range(kinds):
            @pl.when(jnp.logical_and(offsets_ref[0, e, k] == offset, there))
            def _(e=e, k=k, halo=halo):
                total_ref[e] += jnp.dot(halo, blocks_ref[e, k], preferred_element_type=jnp.float32)
    for s, other in enumerate(others):
        g = lax.rem(grid + grids - 1 - s, grids)
        for c in range(donor_ref.shape[3]):
            @pl.when(c < live_ref[0, 0, g])
            def _(g=g, c=c, other=other):
                f = fringe_ref[0, 0, g, c]
                value = other[donor_ref[0, 0, g, c]].astype(jnp.float32)
                total_ref[f] += weight_ref[0, 0, g, c] * value
    for e in range(count):
        v_ref[e] = total_ref[e].astype(jnp.bfloat16)
    side_out[...] = v_ref[core * last]
    chip_out[...] = v_ref[(1 - core) * last]


def gram_kernel(*refs):
    fields, (keep_ref, send_ref) = refs[: S + 1], refs[S + 1 :]
    count, n = fields[0].shape[:2]
    total = None
    for e in range(count):
        rows = jnp.concatenate([f[e] for f in fields], axis=0)
        part = lax.dot_general(rows, rows, (((1,), (1,)), ((), ())), preferred_element_type=jnp.float32)
        total = part if total is None else total + part
    b = lambda i, j0, j1: total[i * n : (i + 1) * n, j0 * n : j1 * n]
    one = jnp.concatenate([b(4, 0, 5), b(3, 0, 3)], axis=1)
    two = jnp.concatenate([b(3, 3, 4), b(2, 0, 3), b(1, 0, 2), b(0, 0, 1), jnp.zeros((n, n), jnp.float32)], axis=1)
    first = lax.axis_index("core") == 0
    keep_ref[...] = jnp.where(first, one, two)
    send_ref[...] = jnp.where(first, two, one)


def factor_kernel(scale, mine_ref, other_ref, r_ref, a_ref):
    first = lax.axis_index("core") == 0
    mine, other = mine_ref[...] * scale, other_ref[...] * scale
    one, two = jnp.where(first, mine, other), jnp.where(first, other, mine)
    n = one.shape[0]
    size = (S + 1) * n
    b = lambda x, j0, j1: x[:, j0 * n : j1 * n]
    wide = lambda x: jnp.concatenate([x, jnp.zeros((n, size - x.shape[1]), jnp.float32)], axis=1) if x.shape[1] < size else x
    low = jnp.concatenate([
        wide(b(two, 6, 7)),
        wide(b(two, 4, 6)),
        wide(b(two, 1, 4)),
        wide(jnp.concatenate([b(one, 5, 8), b(two, 0, 1)], axis=1)),
        b(one, 0, 5),
    ], axis=0)
    row = lax.broadcasted_iota(jnp.int32, (size, size), 0)
    col = lax.broadcasted_iota(jnp.int32, (size, size), 1)
    a = jnp.where(row >= col, low, low.T)
    r = jnp.zeros((size, size), jnp.float32)
    for j in range(size):
        top = a[j : j + 1, :]
        side = a[:, j : j + 1]
        pivot = a[j : j + 1, j : j + 1]
        scaled = top * lax.rsqrt(pivot)
        r = jnp.where(row == j, scaled, r)
        a = a - side * (top / pivot)
    r_ref[...] = jnp.where(col >= row, r, 0.0)


def local(rhs, blocks, offsets, donor_elem, fringe_elem, donor_weight, fringe_count):
    _, elem_count, n, unknowns = rhs.shape
    chips, cores, grids = (lax.axis_size(a) for a in ("chip", "core", "grid"))
    axes = ("chip", "core", "grid")
    at = lambda chip, core, grid: (chip * cores + core) * grids + grid % grids
    side = []
    for g in range(grids):
        for chip in range(chips - 1):
            side += [(at(chip, 1, g), at(chip + 1, 0, g)), (at(chip + 1, 0, g), at(chip, 1, g))]
        side += [(at(0, 0, g), at(0, 0, g + 1)), (at(chips - 1, 1, g), at(chips - 1, 1, g + 1))]
    swap = [(0, 1), (1, 0)]

    def exchange(v, to_side, to_chip):
        others = [
            lax.ppermute(v, "grid", [(g, (g + s) % grids) for g in range(grids)])
            for s in range(1, grids)
        ]
        return lax.ppermute(to_side, axes, side), lax.ppermute(to_chip, "core", swap), others

    halo_type = jax.ShapeDtypeStruct((n, unknowns), jnp.bfloat16)
    field_type = jax.ShapeDtypeStruct((elem_count, n, unknowns), jnp.bfloat16)
    acc_type = jax.ShapeDtypeStruct((elem_count, n, unknowns), jnp.float32)
    half_type = jax.ShapeDtypeStruct((n, 8 * n), jnp.float32)
    limit = pltpu.CompilerParams(vmem_limit_bytes=24 << 20)
    flops = 2 * elem_count * n * unknowns * unknowns * blocks.shape[2]

    field = rhs[0]
    to_side, to_chip = pl.pallas_call(
        edges_kernel, out_shape=(halo_type, halo_type), in_specs=[VMEM], out_specs=(VMEM, VMEM),
        compiler_params=limit, name="edges",
    )(field)
    blocks = pltpu.with_memory_space_constraint(blocks[0], pltpu.VMEM)
    basis = [field]
    for level in range(S):
        from_side, from_chip, others = exchange(field, to_side, to_chip)
        acc = pl.pallas_call(
            inner_kernel, out_shape=acc_type, in_specs=[SMEM, VMEM, VMEM], out_specs=VMEM,
            compiler_params=limit, name="inner",
            cost_estimate=pl.CostEstimate(flops=flops, bytes_accessed=blocks.size * 2, transcendentals=0),
        )(offsets, field, blocks)
        field, to_side, to_chip = pl.pallas_call(
            functools.partial(outer_kernel, grids),
            out_shape=(field_type, halo_type, halo_type),
            in_specs=[SMEM] * 5 + [VMEM] * (4 + grids - 1),
            out_specs=(VMEM, VMEM, VMEM),
            scratch_shapes=[pltpu.VMEM((elem_count, n, unknowns), jnp.float32)],
            compiler_params=limit, name="outer",
        )(offsets, donor_elem, fringe_elem, donor_weight, fringe_count, acc, blocks, from_side, from_chip, *others)
        basis.append(field)
    keep, send = pl.pallas_call(
        gram_kernel, out_shape=(half_type, half_type), in_specs=[VMEM] * (S + 1), out_specs=(VMEM, VMEM),
        compiler_params=limit, name="gram",
    )(*basis)
    half = keep + lax.ppermute(send, "core", swap)
    parts = lax.all_to_all(jnp.broadcast_to(half[None], (chips * grids, n, 8 * n)), ("chip", "grid"), 0, 0, tiled=True)
    mine = parts.sum(axis=0)
    other = lax.ppermute(mine, "core", swap)
    columns = (S + 1) * n
    row_total = grids * chips * cores * elem_count * unknowns
    r_factor = pl.pallas_call(
        functools.partial(factor_kernel, 1.0 / row_total),
        out_shape=jax.ShapeDtypeStruct((columns, columns), jnp.float32),
        in_specs=[VMEM] * 2, out_specs=VMEM,
        scratch_shapes=[pltpu.VMEM((columns, columns), jnp.float32)],
        compiler_params=limit, name="factor",
    )(mine, other)
    powers = jnp.stack(basis[1:], axis=1)[None]
    return (powers, r_factor)


def solution(mesh):
    dom, grids = mesh.shape["dom"], mesh.shape["grid"]
    split = Mesh(mesh.devices.reshape(dom // CORES, CORES, grids), ("chip", "core", "grid"))
    where = ("chip", "core")
    in_specs = (
        P("grid", where, None, None),
        P("grid", where, None, None, None),
        P("grid", where, None),
        P("grid", where, None, None),
        P("grid", where, None, None),
        P("grid", where, None, None),
        P("grid", where, None),
    )
    out_specs = (P("grid", where, None, None, None), P())
    return jax.shard_map(local, mesh=split, in_specs=in_specs, out_specs=out_specs, check_vma=False)
```

```python
import functools

import jax
import jax.numpy as jnp
from jax import lax
from jax.experimental import pallas as pl
from jax.experimental.pallas import tpu as pltpu
from jax.sharding import Mesh
from jax.sharding import PartitionSpec as P

S = 4
H = 1
CORES = 2

VMEM = pl.BlockSpec(memory_space=pltpu.VMEM)
HBM = pl.BlockSpec(memory_space=pltpu.HBM)
SMEM = pl.BlockSpec(memory_space=pltpu.SMEM)


def start_kernel(*refs):
    sources, rest = refs[:6], refs[6:]
    targets, side_ref, chip_ref, sems = rest[:6], rest[6], rest[7], rest[8]
    copies = [pltpu.make_async_copy(a, b, sems.at[i]) for i, (a, b) in enumerate(zip(sources, targets))]
    for copy in copies:
        copy.start()
    copies[0].wait()
    v_ref = targets[0]
    last = v_ref.shape[0] - 1
    core = lax.axis_index("core")
    side_ref[...] = v_ref[core * last]
    chip_ref[...] = v_ref[(1 - core) * last]
    for copy in copies[1:]:
        copy.wait()


def inner_products(offsets_ref, v_ref, chip_ref, acc_ref, block_of):
    count, kinds = v_ref.shape[0], offsets_ref.shape[0]
    core = lax.axis_index("core")
    for e in range(count):
        total = None
        get = block_of(e)
        for k in range(kinds):
            col = e + offsets_ref[k, 0, e]
            inside = jnp.logical_and(col >= 0, col < count)
            lhs = v_ref[jnp.clip(col, 0, count - 1)]
            if e == 0 or e == count - 1:
                halo = jnp.logical_or(
                    jnp.logical_and(col < 0, core == 1), jnp.logical_and(col >= count, core == 0)
                )
                lhs = jnp.where(inside, lhs, jnp.where(halo, chip_ref[...], jnp.zeros_like(lhs)))
            part = jnp.dot(lhs, get(k), preferred_element_type=jnp.float32)
            total = part if total is None else total + part
        acc_ref[e] = total


def first_inner_kernel(offsets_ref, v_ref, chip_ref, source_ref, acc_ref, blocks_ref, sems):
    count = v_ref.shape[0]
    copies = [pltpu.make_async_copy(source_ref.at[e], blocks_ref.at[e], sems.at[e]) for e in range(count)]
    for copy in copies:
        copy.start()

    def block_of(e):
        copies[e].wait()
        return lambda k: blocks_ref[e, k]

    inner_products(offsets_ref, v_ref, chip_ref, acc_ref, block_of)


def inner_kernel(offsets_ref, v_ref, chip_ref, blocks_ref, acc_ref):
    inner_products(offsets_ref, v_ref, chip_ref, acc_ref, lambda e: lambda k: blocks_ref[e, k])


def outer_kernel(
    grids, offsets_ref, donor_ref, fringe_ref, weight_ref, live_ref,
    acc_ref, blocks_ref, halo_ref, *rest
):
    others, (v_ref, *edges, total_ref) = rest[: grids - 1], rest[grids - 1 :]
    count, kinds = blocks_ref.shape[:2]
    last = count - 1
    chips = lax.axis_size("chip")
    chip, core, grid = (lax.axis_index(a) for a in ("chip", "core", "grid"))
    for e in range(count):
        total_ref[e] = acc_ref[e]
    there = jnp.where(core == 0, chip > 0, chip < chips - 1)
    edge = core * last
    total = total_ref[edge]
    for k in range(kinds):
        used = jnp.logical_and(offsets_ref[k, 0, edge] == jnp.where(core == 0, -H, H), there)
        lhs = jnp.where(used, halo_ref[...], jnp.zeros_like(halo_ref))
        total += jnp.dot(lhs, blocks_ref[edge, k], preferred_element_type=jnp.float32)
    total_ref[edge] = total
    for s, other in enumerate(others):
        g = lax.rem(grid + grids - 1 - s, grids)
        for c in range(donor_ref.shape[3]):
            f = fringe_ref[0, 0, g, c]
            weight = jnp.where(c < live_ref[0, 0, g], weight_ref[0, 0, g, c], 0.0)
            total_ref[f] += weight * other[donor_ref[0, 0, g, c]].astype(jnp.float32)
    for e in range(count):
        v_ref[e] = total_ref[e].astype(jnp.bfloat16)
    for edge_ref, edge in zip(edges, (core * last, (1 - core) * last)):
        edge_ref[...] = v_ref[edge]


def gram_kernel(*refs):
    fields, (keep_ref, send_ref) = refs[: S + 1], refs[S + 1 :]
    count, n = fields[0].shape[:2]
    total = None
    for e in range(count):
        rows = jnp.concatenate([f[e] for f in fields], axis=0)
        part = lax.dot_general(rows, rows, (((1,), (1,)), ((), ())), preferred_element_type=jnp.float32)
        total = part if total is None else total + part
    b = lambda i, j0, j1: total[i * n : (i + 1) * n, j0 * n : j1 * n]
    one = jnp.concatenate([b(4, 0, 5), b(3, 0, 3)], axis=1)
    two = jnp.concatenate([b(3, 3, 4), b(2, 0, 3), b(1, 0, 2), b(0, 0, 1), jnp.zeros((n, n), jnp.float32)], axis=1)
    first = lax.axis_index("core") == 0
    keep_ref[...] = jnp.where(first, one, two)
    send_ref[...] = jnp.where(first, two, one)


def cholesky_rows(panels, height, r_ref):
    size = len(panels) * height
    lane = lax.broadcasted_iota(jnp.int32, (1, size), 1)
    panels = list(panels)
    for q in range(len(panels)):
        later = range(q, len(panels))
        wide = lambda p, c: jnp.broadcast_to(panels[p][:, q * height + c : q * height + c + 1], (height, size))
        side = {(c, p): wide(p, c) for c in range(height) for p in later}
        for c in range(0, height, 2):
            one, two = panels[q][c : c + 1], panels[q][c + 1 : c + 2]
            a, b, d = side[c, q][c : c + 1], side[c + 1, q][c : c + 1], side[c + 1, q][c + 1 : c + 2]
            det = a * d - b * b
            inv_det = 1.0 / det
            root = lax.rsqrt(a)
            inv_a = root * root
            j = q * height + c
            r_ref[j : j + 1, :] = jnp.where(lane >= j, one * root, 0.0)
            second = (two - (b * inv_a) * one) * lax.rsqrt(det * inv_a)
            r_ref[j + 1 : j + 2, :] = jnp.where(lane >= j + 1, second, 0.0)
            if c + 2 == height and q + 1 == len(panels):
                break
            tops = [(side[e, q][c : c + 1], side[e, q][c + 1 : c + 2]) for e in range(c + 2, height)]
            for p in later:
                if p == q and c + 2 == height:
                    continue
                x, y = side[c, p], side[c + 1, p]
                w_one, w_two = (d * x - b * y) * inv_det, (a * y - b * x) * inv_det
                panels[p] = panels[p] - w_one * one - w_two * two
                for e, (t_one, t_two) in zip(range(c + 2, height), tops):
                    side[e, p] = side[e, p] - w_one * t_one - w_two * t_two


def factor_kernel(scale, mine_ref, other_ref, r_ref):
    first = lax.axis_index("core") == 0
    mine, other = mine_ref[...] * scale, other_ref[...] * scale
    one, two = jnp.where(first, mine, other), jnp.where(first, other, mine)
    n = one.shape[0]
    size = (S + 1) * n
    b = lambda x, j0, j1: x[:, j0 * n : j1 * n]
    wide = lambda x: jnp.concatenate([x, jnp.zeros((n, size - x.shape[1]), jnp.float32)], axis=1)
    low = jnp.concatenate([
        wide(b(two, 6, 7)),
        wide(b(two, 4, 6)),
        wide(b(two, 1, 4)),
        wide(jnp.concatenate([b(one, 5, 8), b(two, 0, 1)], axis=1)),
        b(one, 0, 5),
    ], axis=0)
    row = lax.broadcasted_iota(jnp.int32, (size, size), 0)
    col = lax.broadcasted_iota(jnp.int32, (size, size), 1)
    a = jnp.where(row >= col, low, low.T)
    height = 8
    cholesky_rows([a[i : i + height] for i in range(0, size, height)], height, r_ref)


def local(rhs, blocks, offsets, donor_elem, fringe_elem, donor_weight, fringe_count):
    _, elem_count, n, unknowns = rhs.shape
    chips, cores, grids = (lax.axis_size(a) for a in ("chip", "core", "grid"))
    axes = ("chip", "core", "grid")
    at = lambda chip, core, grid: (chip * cores + core) * grids + grid % grids
    side = []
    for g in range(grids):
        for chip in range(chips - 1):
            side += [(at(chip, 1, g), at(chip + 1, 0, g)), (at(chip + 1, 0, g), at(chip, 1, g))]
        side += [(at(0, 0, g), at(0, 0, g + 1)), (at(chips - 1, 1, g), at(chips - 1, 1, g + 1))]
    swap = [(0, 1), (1, 0)]

    def exchange(v, to_side, to_chip):
        from_chip = lax.ppermute(to_chip, "core", swap)
        others = [
            lax.ppermute(v, "grid", [(g, (g + s) % grids) for g in range(grids)])
            for s in range(1, grids)
        ]
        return lax.ppermute(to_side, axes, side), from_chip, others

    halo_type = jax.ShapeDtypeStruct((n, unknowns), jnp.bfloat16)
    field_type = jax.ShapeDtypeStruct((elem_count, n, unknowns), jnp.bfloat16)
    acc_type = jax.ShapeDtypeStruct((elem_count, n, unknowns), jnp.float32)
    half_type = jax.ShapeDtypeStruct((n, 8 * n), jnp.float32)
    limit = pltpu.CompilerParams(vmem_limit_bytes=24 << 20)
    flops = 2 * elem_count * n * unknowns * unknowns * blocks.shape[2]

    kinds = blocks.shape[2]
    by_kind = jnp.transpose(offsets, (2, 0, 1))
    small = (by_kind, donor_elem, fringe_elem, donor_weight, fringe_count)
    field, *small, side_edge, chip_edge = pl.pallas_call(
        start_kernel,
        out_shape=(field_type, *(pltpu.SMEM(x.shape, x.dtype) for x in small), halo_type, halo_type),
        in_specs=[HBM] * 6, out_specs=(VMEM, *[SMEM] * 5, VMEM, VMEM),
        scratch_shapes=[pltpu.SemaphoreType.DMA((6,))],
        compiler_params=limit, name="start",
    )(*(pltpu.with_memory_space_constraint(x, pltpu.HBM) for x in (rhs[0], *small)))
    edges = (side_edge, chip_edge)
    basis = [field]
    stored = None
    for level in range(S):
        from_side, from_chip, others = exchange(field, *edges)
        cost = pl.CostEstimate(flops=flops, bytes_accessed=blocks.size * 2, transcendentals=0)
        if level == 0:
            acc, stored = pl.pallas_call(
                first_inner_kernel,
                out_shape=(acc_type, pltpu.VMEM(blocks.shape[1:], blocks.dtype)),
                in_specs=[SMEM, VMEM, VMEM, HBM], out_specs=(VMEM, VMEM),
                scratch_shapes=[pltpu.SemaphoreType.DMA((elem_count,))],
                compiler_params=limit, name="first_inner", cost_estimate=cost,
            )(small[0], field, from_chip, pltpu.with_memory_space_constraint(blocks[0], pltpu.HBM))
        else:
            acc = pl.pallas_call(
                inner_kernel, out_shape=acc_type, in_specs=[SMEM, VMEM, VMEM, VMEM], out_specs=VMEM,
                compiler_params=limit, name="inner", cost_estimate=cost,
            )(small[0], field, from_chip, stored)
        edges = 2 if level + 1 < S else 0
        field, *edges = pl.pallas_call(
            functools.partial(outer_kernel, grids),
            out_shape=(field_type, *[halo_type] * edges),
            in_specs=[SMEM] * 5 + [VMEM] * (3 + grids - 1),
            out_specs=(VMEM, *[VMEM] * edges),
            scratch_shapes=[pltpu.VMEM((elem_count, n, unknowns), jnp.float32)],
            compiler_params=limit, name="outer",
        )(*small, acc, stored, from_side, *others)
        basis.append(field)
    keep, send = pl.pallas_call(
        gram_kernel, out_shape=(half_type, half_type), in_specs=[VMEM] * (S + 1), out_specs=(VMEM, VMEM),
        compiler_params=limit, name="gram",
    )(*basis)
    half = keep + lax.ppermute(send, "core", swap)
    parts = lax.all_to_all(jnp.broadcast_to(half[None], (chips * grids, n, 8 * n)), ("chip", "grid"), 0, 0, tiled=True)
    mine = parts.sum(axis=0)
    other = lax.ppermute(mine, "core", swap)
    columns = (S + 1) * n
    row_total = grids * chips * cores * elem_count * unknowns
    r_factor = pl.pallas_call(
        functools.partial(factor_kernel, 1.0 / row_total),
        out_shape=jax.ShapeDtypeStruct((columns, columns), jnp.float32),
        in_specs=[VMEM] * 2, out_specs=VMEM,
        compiler_params=limit, name="factor",
    )(mine, other)
    powers = jnp.stack(basis[1:], axis=1)[None]
    return (powers, r_factor)


def solution(mesh):
    dom, grids = mesh.shape["dom"], mesh.shape["grid"]
    split = Mesh(mesh.devices.reshape(dom // CORES, CORES, grids), ("chip", "core", "grid"))
    where = ("chip", "core")
    in_specs = (
        P("grid", where, None, None),
        P("grid", where, None, None, None),
        P("grid", where, None),
        P("grid", where, None, None),
        P("grid", where, None, None),
        P("grid", where, None, None),
        P("grid", where, None),
    )
    out_specs = (P("grid", where, None, None, None), P())
    return jax.shard_map(local, mesh=split, in_specs=in_specs, out_specs=out_specs, check_vma=False)
```

```python
import functools

import jax
import jax.numpy as jnp
from jax import lax
from jax.experimental import pallas as pl
from jax.experimental.pallas import tpu as pltpu
from jax.sharding import Mesh
from jax.sharding import PartitionSpec as P

S = 4
H = 1
CORES = 2

VMEM = pl.BlockSpec(memory_space=pltpu.VMEM)
HBM = pl.BlockSpec(memory_space=pltpu.HBM)
SMEM = pl.BlockSpec(memory_space=pltpu.SMEM)


def start_kernel(*refs):
    sources, rest = refs[:6], refs[6:]
    targets, side_ref, chip_ref, sems = rest[:6], rest[6], rest[7], rest[8]
    field_ref = targets[0]
    count = field_ref.shape[0] - 1
    targets = (field_ref.at[pl.ds(0, count)], *targets[1:])
    copies = [pltpu.make_async_copy(a, b, sems.at[i]) for i, (a, b) in enumerate(zip(sources, targets))]
    for copy in copies:
        copy.start()
    copies[0].wait()
    core = lax.axis_index("core")
    near, far = field_ref[core * (count - 1)], field_ref[(1 - core) * (count - 1)]
    side_ref[0] = near
    side_ref[1] = far
    chip_ref[...] = far
    for copy in copies[1:]:
        copy.wait()
    donor_ref = targets[2]
    _, _, grids, slots = donor_ref.shape
    row = lax.broadcasted_iota(jnp.int32, field_ref.shape[1:], 0)
    asked = jnp.zeros(field_ref.shape[1:], jnp.int32)
    for g in range(grids):
        for c in range(slots):
            asked = jnp.where(row == g * slots + c, donor_ref[0, 0, g, c], asked)
    field_ref[count] = asked.astype(jnp.float32).astype(jnp.bfloat16)


def inner_kernel(offsets_ref, v_ref, chip_ref, blocks_ref, acc_ref):
    count, kinds = acc_ref.shape[0], offsets_ref.shape[0]
    core = lax.axis_index("core")
    for e in range(count):
        total = None
        for k in range(kinds):
            col = e + offsets_ref[k, 0, e]
            inside = jnp.logical_and(col >= 0, col < count)
            lhs = v_ref[jnp.clip(col, 0, count - 1)]
            if e == 0 or e == count - 1:
                halo = jnp.logical_or(
                    jnp.logical_and(col < 0, core == 1), jnp.logical_and(col >= count, core == 0)
                )
                lhs = jnp.where(inside, lhs, jnp.where(halo, chip_ref[...], jnp.zeros_like(lhs)))
            part = jnp.dot(lhs, blocks_ref[e, k], preferred_element_type=jnp.float32)
            total = part if total is None else total + part
        acc_ref[e] = total


def outer_kernel(
    grids, first, last_level, offsets_ref, donor_ref, fringe_ref, weight_ref, live_ref,
    acc_ref, blocks_ref, halo_ref, *rest
):
    take = lambda m: (rest[:m], rest[m:])
    asked, rest = take(grids - 1)
    others, rest = (asked, rest) if first else take(grids - 1)
    v_ref, *sends, total_ref = rest
    count, kinds = blocks_ref.shape[:2]
    slots = donor_ref.shape[3]
    last = count - 1
    chips = lax.axis_size("chip")
    chip, core, grid = (lax.axis_index(a) for a in ("chip", "core", "grid"))
    for e in range(count):
        total_ref[e] = acc_ref[e]
    there = jnp.where(core == 0, chip > 0, chip < chips - 1)
    edge = core * last
    total = total_ref[edge]
    for k in range(kinds):
        used = jnp.logical_and(offsets_ref[k, 0, edge] == jnp.where(core == 0, -H, H), there)
        lhs = jnp.where(used, halo_ref[0], jnp.zeros(halo_ref.shape[1:], halo_ref.dtype))
        total += jnp.dot(lhs, blocks_ref[edge, k], preferred_element_type=jnp.float32)
    total_ref[edge] = total
    for s, other in enumerate(others):
        g = lax.rem(grid + grids - 1 - s, grids)
        for c in range(slots):
            f = fringe_ref[0, 0, g, c]
            weight = jnp.where(c < live_ref[0, 0, g], weight_ref[0, 0, g, c], 0.0)
            value = other[donor_ref[0, 0, g, c] if first else c].astype(jnp.float32)
            total_ref[f] += weight * value
    for e in range(count):
        v_ref[e] = total_ref[e].astype(jnp.bfloat16)
    if last_level:
        return
    sends[0][0] = v_ref[edge]
    sends[0][1] = v_ref[last - edge]
    sends[1][...] = v_ref[last - edge]
    row = lax.broadcasted_iota(jnp.int32, v_ref.shape[1:], 0)
    for s, send_ref in enumerate(sends[2:]):
        wish = asked[grids - 2 - s][count].astype(jnp.float32)
        for c in range(slots):
            index = jnp.sum(jnp.where(row == grid * slots + c, wish, 0.0), axis=0, keepdims=True)
            picked = total_ref[0]
            for e in range(1, count):
                picked = jnp.where(index == e, total_ref[e], picked)
            send_ref[c] = picked.astype(jnp.bfloat16)


def stripe(fields, upto):
    count = fields[1].shape[0]
    total = None
    for e in range(count):
        rows = jnp.concatenate([f[e] for f in fields[: upto + 1]], axis=0)
        part = lax.dot_general(
            fields[upto][e], rows, (((1,), (1,)), ((), ())), preferred_element_type=jnp.float32
        )
        total = part if total is None else total + part
    return total


def early_gram_kernel(*refs):
    fields, (early_ref,) = refs[:S], refs[S:]
    n = early_ref.shape[0]
    total = None
    for e in range(fields[1].shape[0]):
        rows = jnp.concatenate([f[e] for f in fields], axis=0)
        part = lax.dot_general(rows, rows, (((1,), (1,)), ((), ())), preferred_element_type=jnp.float32)
        total = part if total is None else total + part
    b = lambda i, j0, j1: total[i * n : (i + 1) * n, j0 * n : j1 * n]
    blank = jnp.zeros((n, n), jnp.float32)
    early_ref[...] = jnp.concatenate(
        [b(3, 0, 3), b(3, 3, 4), b(2, 0, 3), b(1, 0, 2), b(0, 0, 1), blank], axis=1
    )


def late_gram_kernel(*refs):
    fields, (early_ref, keep_ref, send_ref) = refs[: S + 1], refs[S + 1 :]
    n = early_ref.shape[0]
    one = jnp.concatenate([stripe(fields, S), early_ref[:, : 3 * n]], axis=1)
    two = early_ref[:, 3 * n :]
    first = lax.axis_index("core") == 0
    keep_ref[...] = jnp.where(first, one, two)
    send_ref[...] = jnp.where(first, two, one)


def cholesky_rows(panels, height, r_ref):
    size = len(panels) * height
    count = len(panels)
    lane = lax.broadcasted_iota(jnp.int32, (height, size), 1)
    sub = lax.broadcasted_iota(jnp.int32, (height, size), 0)
    panels = list(panels)
    row = lambda x, c: jnp.broadcast_to(x[c : c + 1], (height, size))
    wide = lambda p, j: jnp.broadcast_to(panels[p][:, j : j + 1], (height, size))
    ahead = {c: wide(0, c) for c in range(height)}
    for q in range(count):
        base = q * height
        more = 2 * height if q + 1 < count else height
        side = {(c, p): wide(p, base + c) for c in range(height) for p in range(q + 1, count)}
        side.update({(c, q): ahead[c] for c in range(height)})
        if q + 1 < count:
            side.update({(c, p): wide(p, base + c) for c in range(height, more) for p in (q, q + 1)})
        out = jnp.zeros((height, size), jnp.float32)
        for c in range(height):
            one = row(panels[q], c)
            a = row(side[c, q], c)
            inv = 1.0 / a
            out = jnp.where(sub == c, one * lax.rsqrt(a), out)
            if c + 1 == height and q + 1 == count:
                break
            tops = {e: row(side[e, q], c) for e in range(c + 1, more)}
            scaled = one * inv
            for p in range(q, count):
                if p == q and c + 1 == height:
                    continue
                x = side[c, p] * inv
                panels[p] = panels[p] - x * one
                for e in range(c + 1, more):
                    if (e, p) in side:
                        side[e, p] = side[e, p] - x * tops[e]
        ahead = {c: side[height + c, q + 1] for c in range(height)} if q + 1 < count else {}
        r_ref[base : base + height, :] = jnp.where(lane >= sub + base, out, 0.0)


def factor_kernel(scale, mine_ref, other_ref, r_ref):
    first = lax.axis_index("core") == 0
    mine, other = mine_ref[...] * scale, other_ref[...] * scale
    one, two = jnp.where(first, mine, other), jnp.where(first, other, mine)
    n = one.shape[0]
    size = (S + 1) * n
    b = lambda x, j0, j1: x[:, j0 * n : j1 * n]
    wide = lambda x: jnp.concatenate([x, jnp.zeros((n, size - x.shape[1]), jnp.float32)], axis=1)
    low = jnp.concatenate([
        wide(b(two, 6, 7)),
        wide(b(two, 4, 6)),
        wide(b(two, 1, 4)),
        wide(jnp.concatenate([b(one, 5, 8), b(two, 0, 1)], axis=1)),
        b(one, 0, 5),
    ], axis=0)
    row = lax.broadcasted_iota(jnp.int32, (size, size), 0)
    col = lax.broadcasted_iota(jnp.int32, (size, size), 1)
    a = jnp.where(row >= col, low, low.T)
    height = 8
    cholesky_rows([a[i : i + height] for i in range(0, size, height)], height, r_ref)


def local(rhs, blocks, offsets, donor_elem, fringe_elem, donor_weight, fringe_count):
    _, elem_count, n, unknowns = rhs.shape
    chips, cores, grids = (lax.axis_size(a) for a in ("chip", "core", "grid"))
    axes = ("chip", "core", "grid")
    at = lambda chip, core, grid: (chip * cores + core) * grids + grid % grids
    side = []
    for g in range(grids):
        for chip in range(chips - 1):
            side += [(at(chip, 1, g), at(chip + 1, 0, g)), (at(chip + 1, 0, g), at(chip, 1, g))]
        side += [(at(0, 0, g), at(0, 0, g + 1)), (at(chips - 1, 1, g), at(chips - 1, 1, g + 1))]
    swap = [(0, 1), (1, 0)]

    def exchange(to_side, to_chip, *donors):
        from_side = lax.ppermute(to_side, axes, side)
        others = [
            lax.ppermute(v, "grid", [(g, (g + s) % grids) for g in range(grids)])
            for s, v in enumerate(donors, 1)
        ]
        return from_side, lax.ppermute(to_chip, "core", swap), others

    halo_type = jax.ShapeDtypeStruct((n, unknowns), jnp.bfloat16)
    side_type = jax.ShapeDtypeStruct((2, n, unknowns), jnp.bfloat16)
    field_type = jax.ShapeDtypeStruct((elem_count, n, unknowns), jnp.bfloat16)
    acc_type = jax.ShapeDtypeStruct((elem_count, n, unknowns), jnp.float32)
    half_type = jax.ShapeDtypeStruct((n, 8 * n), jnp.float32)
    limit = pltpu.CompilerParams(vmem_limit_bytes=24 << 20)
    flops = 2 * elem_count * n * unknowns * unknowns * blocks.shape[2]

    kinds = blocks.shape[2]
    by_kind = jnp.transpose(offsets, (2, 0, 1))
    small = (by_kind, donor_elem, fringe_elem, donor_weight, fringe_count)
    field, *small, side_edge, chip_edge = pl.pallas_call(
        start_kernel,
        out_shape=(
            jax.ShapeDtypeStruct((elem_count + 1, n, unknowns), jnp.bfloat16),
            *(pltpu.SMEM(x.shape, x.dtype) for x in small), side_type, halo_type,
        ),
        in_specs=[HBM] * 6, out_specs=(VMEM, *[SMEM] * 5, VMEM, VMEM),
        scratch_shapes=[pltpu.SemaphoreType.DMA((6,))],
        compiler_params=limit, name="start",
        cost_estimate=pl.CostEstimate(flops=4 * 10**9, bytes_accessed=10**7, transcendentals=0),
    )(*(pltpu.with_memory_space_constraint(x, pltpu.HBM) for x in (rhs[0], *small)))
    sends = (side_edge, chip_edge, *[field] * (grids - 1))
    donor_type = jax.ShapeDtypeStruct((donor_elem.shape[3], n, unknowns), jnp.bfloat16)
    asked = []
    basis = [field]
    blocks = blocks[0]
    for level in range(S):
        from_side, from_chip, others = exchange(*sends)
        cost = pl.CostEstimate(flops=flops, bytes_accessed=blocks.size * 2, transcendentals=0)
        acc = pl.pallas_call(
            inner_kernel, out_shape=acc_type, in_specs=[SMEM, VMEM, VMEM, VMEM], out_specs=VMEM,
            compiler_params=limit, name="inner", cost_estimate=cost,
        )(small[0], field, from_chip, blocks)
        if level + 1 == S:
            early = pl.pallas_call(
                early_gram_kernel, out_shape=jax.ShapeDtypeStruct((n, 11 * n), jnp.float32),
                in_specs=[VMEM] * S, out_specs=VMEM, compiler_params=limit, name="early_gram", cost_estimate=cost,
            )(*basis)
        types = () if level + 1 == S else (side_type, halo_type, *[donor_type] * (grids - 1))
        messages = [*asked, *others]
        field, *sends = pl.pallas_call(
            functools.partial(outer_kernel, grids, level == 0, level + 1 == S),
            out_shape=(field_type, *types),
            in_specs=[SMEM] * 5 + [VMEM] * (3 + len(messages)),
            out_specs=(VMEM, *[VMEM] * len(types)),
            scratch_shapes=[pltpu.VMEM((elem_count, n, unknowns), jnp.float32)],
            compiler_params=limit, name="outer",
        )(*small, acc, blocks, from_side, *messages)
        asked = asked or others
        basis.append(field)
    keep, send = pl.pallas_call(
        late_gram_kernel, out_shape=(half_type, half_type), in_specs=[VMEM] * (S + 2), out_specs=(VMEM, VMEM),
        compiler_params=limit, name="late_gram",
    )(*basis, early)
    half = keep + lax.ppermute(send, "core", swap)
    parts = lax.all_to_all(jnp.broadcast_to(half[None], (chips * grids, n, 8 * n)), ("chip", "grid"), 0, 0, tiled=True)
    mine = parts.sum(axis=0)
    other = lax.ppermute(mine, "core", swap)
    columns = (S + 1) * n
    row_total = grids * chips * cores * elem_count * unknowns
    r_factor = pl.pallas_call(
        functools.partial(factor_kernel, 1.0 / row_total),
        out_shape=jax.ShapeDtypeStruct((columns, columns), jnp.float32),
        in_specs=[VMEM] * 2, out_specs=VMEM,
        compiler_params=limit, name="factor",
    )(mine, other)
    powers = jnp.stack(basis[1:], axis=1)[None]
    return (powers, r_factor)


def solution(mesh):
    dom, grids = mesh.shape["dom"], mesh.shape["grid"]
    split = Mesh(mesh.devices.reshape(dom // CORES, CORES, grids), ("chip", "core", "grid"))
    where = ("chip", "core")
    in_specs = (
        P("grid", where, None, None),
        P("grid", where, None, None, None),
        P("grid", where, None),
        P("grid", where, None, None),
        P("grid", where, None, None),
        P("grid", where, None, None),
        P("grid", where, None),
    )
    out_specs = (P("grid", where, None, None, None), P())
    return jax.shard_map(local, mesh=split, in_specs=in_specs, out_specs=out_specs, check_vma=False)
```

```python
import functools

import jax
import jax.numpy as jnp
from jax import lax
from jax.experimental import pallas as pl
from jax.experimental.pallas import tpu as pltpu
from jax.sharding import Mesh
from jax.sharding import PartitionSpec as P

S = 4
H = 1
CORES = 2

VMEM = pl.BlockSpec(memory_space=pltpu.VMEM)
HBM = pl.BlockSpec(memory_space=pltpu.HBM)
SMEM = pl.BlockSpec(memory_space=pltpu.SMEM)


def start_kernel(*refs):
    half = len(refs) // 2
    sems = refs[-1]
    copies = [pltpu.make_async_copy(a, b, sems.at[i]) for i, (a, b) in enumerate(zip(refs[:half], refs[half:-1]))]
    for copy in copies:
        copy.start()
    for copy in copies:
        copy.wait()


def inner_kernel(offsets_ref, v_ref, chip_ref, blocks_ref, acc_ref):
    count, kinds = blocks_ref.shape[:2]
    core = lax.axis_index("core")
    halo = chip_ref[core * (count - 1)] if len(chip_ref.shape) == 3 else chip_ref[...]
    for e in range(count):
        total = None
        for k in range(kinds):
            col = e + offsets_ref[k, 0, e]
            inside = jnp.logical_and(col >= 0, col < count)
            lhs = v_ref[jnp.clip(col, 0, count - 1)]
            if e == 0 or e == count - 1:
                near = jnp.logical_or(
                    jnp.logical_and(col < 0, core == 1), jnp.logical_and(col >= count, core == 0)
                )
                lhs = jnp.where(inside, lhs, jnp.where(near, halo, jnp.zeros_like(lhs)))
            part = jnp.dot(lhs, blocks_ref[e, k], preferred_element_type=jnp.float32)
            total = part if total is None else total + part
        acc_ref[e] = total


def next_field(
    grids, first, offsets_ref, donor_ref, fringe_ref, weight_ref, live_ref, acc_ref, blocks_ref, halo_ref, others
):
    count, kinds = blocks_ref.shape[:2]
    last = count - 1
    chips = lax.axis_size("chip")
    chip, core, grid = (lax.axis_index(a) for a in ("chip", "core", "grid"))
    there = jnp.where(core == 0, chip > 0, chip < chips - 1)
    edge = core * last
    halo = halo_ref[last - edge] if first else halo_ref[0]
    product = None
    for k in range(kinds):
        used = jnp.logical_and(offsets_ref[k, 0, edge] == jnp.where(core == 0, -H, H), there)
        lhs = jnp.where(used, halo, jnp.zeros_like(halo))
        part = jnp.dot(lhs, blocks_ref[edge, k], preferred_element_type=jnp.float32)
        product = part if product is None else product + part
    totals = [acc_ref[e] for e in range(count)]
    for s, other in enumerate(others):
        g = lax.rem(grid + grids - 1 - s, grids)
        for c in range(donor_ref.shape[3]):
            target = jnp.where(c < live_ref[0, 0, g], fringe_ref[0, 0, g, c], -1)
            weight = weight_ref[0, 0, g, c]
            value = other[donor_ref[0, 0, g, c] if first else c].astype(jnp.float32)
            for e in range(count):
                totals[e] = totals[e] + jnp.where(target == e, weight, 0.0) * value
    for e in {0, last}:
        totals[e] = totals[e] + jnp.where(edge == e, product, jnp.zeros_like(product))
    return totals


def outer_kernel(grids, first, *refs):
    take = lambda refs, m: (refs[:m], refs[m:])
    shared, rest = take(refs, 7)
    halo, rest = ((), rest) if first else take(rest, 1)
    asked, rest = take(rest, grids - 1)
    others, rest = take(rest, grids - 1)
    halo, rest = take(rest, 1) if first else (halo, rest)
    v_ref, side_ref, chip_ref, *sends = rest
    totals = next_field(grids, first, *shared, *halo, others)
    count = len(totals)
    fields = [t.astype(jnp.bfloat16) for t in totals]
    for e in range(count):
        v_ref[e] = fields[e]
    start = lax.axis_index("core") == 0
    near, far = (jnp.where(start, *pair) for pair in ((fields[0], fields[-1]), (fields[-1], fields[0])))
    side_ref[0] = near
    side_ref[1] = far
    chip_ref[...] = far
    row = lax.broadcasted_iota(jnp.int32, asked[0].shape[2:], 0) if asked else None
    for s, send_ref in enumerate(sends):
        wish = jnp.where(row == lax.axis_index("grid"), asked[grids - 2 - s][0, 0], 0)
        wish = jnp.sum(wish.astype(jnp.float32), axis=0, keepdims=True)
        for c in range(send_ref.shape[0]):
            index = jnp.broadcast_to(wish[:, c : c + 1], totals[0].shape)
            picked = totals[0]
            for e in range(1, count):
                picked = jnp.where(index == e, totals[e], picked)
            send_ref[c] = picked.astype(jnp.bfloat16)


def early_gram_kernel(*refs):
    fields, (one_ref, two_ref) = refs[:S], refs[S:]
    count, n = fields[0].shape[:2]
    total = None
    for e in range(count):
        rows = jnp.concatenate([f[e] for f in fields], axis=0)
        part = lax.dot_general(rows, rows, (((1,), (1,)), ((), ())), preferred_element_type=jnp.float32)
        total = part if total is None else total + part
    b = lambda i, j0, j1: total[i * n : (i + 1) * n, j0 * n : j1 * n]
    blank = jnp.zeros((n, n), jnp.float32)
    one_ref[...] = jnp.concatenate([*[blank] * (S + 1), b(3, 0, 3)], axis=1)
    two_ref[...] = jnp.concatenate([b(3, 3, 4), b(2, 0, 3), b(1, 0, 2), b(0, 0, 1), blank], axis=1)


def last_kernel(grids, *refs):
    shared, rest = refs[:8], refs[8:]
    others, rest = rest[: grids - 1], rest[grids - 1 :]
    fields, (one_ref, two_ref, v_ref, keep_ref, send_ref) = rest[:S], rest[S:]
    n, width = one_ref.shape
    total = None
    for e, values in enumerate(next_field(grids, False, *shared, others)):
        power = values.astype(jnp.bfloat16)
        v_ref[e] = power
        blank = jnp.zeros((width - (S + 1) * n, power.shape[1]), power.dtype)
        rows = jnp.concatenate([*[f[e] for f in fields], power, blank], axis=0)
        part = lax.dot_general(power, rows, (((1,), (1,)), ((), ())), preferred_element_type=jnp.float32)
        total = part if total is None else total + part
    one, two = total + one_ref[...], two_ref[...]
    first = lax.axis_index("core") == 0
    keep_ref[...] = jnp.where(first, one, two)
    send_ref[...] = jnp.where(first, two, one)


def cholesky_rows(panels, height, r_ref):
    size = len(panels) * height
    count = len(panels)
    lane = lax.broadcasted_iota(jnp.int32, (height, size), 1)
    sub = lax.broadcasted_iota(jnp.int32, (height, size), 0)
    panels = list(panels)
    row = lambda x, c: jnp.broadcast_to(x[c : c + 1], (height, size))
    wide = lambda p, j: jnp.broadcast_to(panels[p][:, j : j + 1], (height, size))
    ahead = {c: wide(0, c) for c in range(height)}
    for q in range(count):
        base = q * height
        more = 2 * height if q + 1 < count else height
        side = {(c, p): wide(p, base + c) for c in range(height) for p in range(q + 1, count)}
        side.update({(c, q): ahead[c] for c in range(height)})
        if q + 1 < count:
            side.update({(c, p): wide(p, base + c) for c in range(height, more) for p in (q, q + 1)})
        out = jnp.zeros((height, size), jnp.float32)
        for c in range(height):
            one = row(panels[q], c)
            a = row(side[c, q], c)
            inv = 1.0 / a
            out = jnp.where(sub == c, one * lax.rsqrt(a), out)
            if c + 1 == height and q + 1 == count:
                break
            tops = {e: row(side[e, q], c) for e in range(c + 1, more)}
            scaled = one * inv
            for p in range(q, count):
                if p == q and c + 1 == height:
                    continue
                x = side[c, p] * inv
                panels[p] = panels[p] - x * one
                for e in range(c + 1, more):
                    if (e, p) in side:
                        side[e, p] = side[e, p] - x * tops[e]
        ahead = {c: side[height + c, q + 1] for c in range(height)} if q + 1 < count else {}
        r_ref[base : base + height, :] = jnp.where(lane >= sub + base, out, 0.0)


def factor_kernel(scale, mine_ref, other_ref, r_ref):
    first = lax.axis_index("core") == 0
    mine, other = mine_ref[...] * scale, other_ref[...] * scale
    one, two = jnp.where(first, mine, other), jnp.where(first, other, mine)
    n = one.shape[0]
    size = (S + 1) * n
    b = lambda x, j0, j1: x[:, j0 * n : j1 * n]
    wide = lambda x: jnp.concatenate([x, jnp.zeros((n, size - x.shape[1]), jnp.float32)], axis=1)
    low = jnp.concatenate([
        wide(b(two, 6, 7)),
        wide(b(two, 4, 6)),
        wide(b(two, 1, 4)),
        wide(jnp.concatenate([b(one, 5, 8), b(two, 0, 1)], axis=1)),
        b(one, 0, 5),
    ], axis=0)
    row = lax.broadcasted_iota(jnp.int32, (size, size), 0)
    col = lax.broadcasted_iota(jnp.int32, (size, size), 1)
    a = jnp.where(row >= col, low, low.T)
    height = 8
    cholesky_rows([a[i : i + height] for i in range(0, size, height)], height, r_ref)


def local(rhs, blocks, offsets, donor_elem, fringe_elem, donor_weight, fringe_count):
    _, elem_count, n, unknowns = rhs.shape
    chips, cores, grids = (lax.axis_size(a) for a in ("chip", "core", "grid"))
    axes = ("chip", "core", "grid")
    at = lambda chip, core, grid: (chip * cores + core) * grids + grid % grids
    side = []
    for g in range(grids):
        for chip in range(chips - 1):
            side += [(at(chip, 1, g), at(chip + 1, 0, g)), (at(chip + 1, 0, g), at(chip, 1, g))]
        side += [(at(0, 0, g), at(0, 0, g + 1)), (at(chips - 1, 1, g), at(chips - 1, 1, g + 1))]
    swap = [(0, 1), (1, 0)]

    around = [[(g, (g + s) % grids) for g in range(grids)] for s in range(1, grids)]

    def exchange(to_side, to_chip, *to_grids):
        from_side = lax.ppermute(to_side, axes, side)
        others = [lax.ppermute(v, "grid", pairs) for v, pairs in zip(to_grids, around)]
        return from_side, lax.ppermute(to_chip, "core", swap), others

    slots = donor_elem.shape[3]
    halo_type = jax.ShapeDtypeStruct((n, unknowns), jnp.bfloat16)
    side_type = jax.ShapeDtypeStruct((2, n, unknowns), jnp.bfloat16)
    donor_type = jax.ShapeDtypeStruct((slots, n, unknowns), jnp.bfloat16)
    field_type = jax.ShapeDtypeStruct((elem_count, n, unknowns), jnp.bfloat16)
    acc_type = jax.ShapeDtypeStruct((elem_count, n, unknowns), jnp.float32)
    half_type = jax.ShapeDtypeStruct((n, 8 * n), jnp.float32)
    limit = pltpu.CompilerParams(vmem_limit_bytes=24 << 20)
    rhs, blocks = rhs[0], blocks[0]
    flops = 2 * blocks.size * n
    cost = pl.CostEstimate(flops=flops, bytes_accessed=blocks.size * 2, transcendentals=0)

    small = (jnp.transpose(offsets, (2, 0, 1)), donor_elem, fringe_elem, donor_weight, fringe_count)
    messages = exchange(rhs, rhs, *[rhs] * (grids - 1))
    asked = [lax.ppermute(donor_elem, "grid", pairs) for pairs in around]
    field, *small = pl.pallas_call(
        start_kernel,
        out_shape=(field_type, *(pltpu.SMEM(x.shape, x.dtype) for x in small)),
        in_specs=[HBM] * 6, out_specs=(VMEM, *[SMEM] * 5),
        scratch_shapes=[pltpu.SemaphoreType.DMA((6,))],
        compiler_params=limit, name="start",
        cost_estimate=pl.CostEstimate(flops=2 * 10**9, bytes_accessed=10**6, transcendentals=0),
    )(*(pltpu.with_memory_space_constraint(x, pltpu.HBM) for x in (rhs, *small)))
    basis = [field]
    for level in range(S):
        from_side, from_chip, others = messages
        acc = pl.pallas_call(
            inner_kernel, out_shape=acc_type, in_specs=[SMEM, VMEM, VMEM, VMEM], out_specs=VMEM,
            compiler_params=limit, name="inner", cost_estimate=cost,
        )(small[0], field, from_chip, blocks)
        shared = (*small, acc, blocks)
        if level + 1 < S:
            field, *sends = pl.pallas_call(
                functools.partial(outer_kernel, grids, level == 0),
                out_shape=(field_type, side_type, halo_type, *[donor_type] * (grids - 1)),
                in_specs=[SMEM] * 5 + [VMEM] * (3 + 2 * (grids - 1)),
                out_specs=(VMEM,) * (3 + grids - 1),
                compiler_params=limit, name="outer",
            )(*shared, *((*asked, *others, from_side) if level == 0 else (from_side, *asked, *others)))
            messages = exchange(*sends)
        else:
            early = pl.pallas_call(
                early_gram_kernel, out_shape=(half_type, half_type),
                in_specs=[VMEM] * S, out_specs=(VMEM, VMEM), compiler_params=limit, name="early_gram", cost_estimate=cost,
            )(*basis)
            field, keep, send = pl.pallas_call(
                functools.partial(last_kernel, grids), out_shape=(field_type, half_type, half_type),
                in_specs=[SMEM] * 5 + [VMEM] * (3 + grids - 1 + S + 2), out_specs=(VMEM,) * 3,
                compiler_params=limit, name="last",
            )(*shared, from_side, *others, *basis, *early)
        basis.append(field)
    half = keep + lax.ppermute(send, "core", swap)
    parts = lax.all_to_all(jnp.broadcast_to(half[None], (chips * grids, n, 8 * n)), ("chip", "grid"), 0, 0, tiled=True)
    mine = parts.sum(axis=0)
    other = lax.ppermute(mine, "core", swap)
    columns = (S + 1) * n
    row_total = grids * chips * cores * elem_count * unknowns
    r_factor = pl.pallas_call(
        functools.partial(factor_kernel, 1.0 / row_total),
        out_shape=jax.ShapeDtypeStruct((columns, columns), jnp.float32),
        in_specs=[VMEM] * 2, out_specs=VMEM,
        compiler_params=limit, name="factor",
    )(mine, other)
    powers = jnp.stack(basis[1:], axis=1)[None]
    return (powers, r_factor)


def solution(mesh):
    dom, grids = mesh.shape["dom"], mesh.shape["grid"]
    split = Mesh(mesh.devices.reshape(dom // CORES, CORES, grids), ("chip", "core", "grid"))
    where = ("chip", "core")
    in_specs = (
        P("grid", where, None, None),
        P("grid", where, None, None, None),
        P("grid", where, None),
        P("grid", where, None, None),
        P("grid", where, None, None),
        P("grid", where, None, None),
        P("grid", where, None),
    )
    out_specs = (P("grid", where, None, None, None), P())
    return jax.shard_map(local, mesh=split, in_specs=in_specs, out_specs=out_specs, check_vma=False)
```

```python
import functools

import jax
import jax.numpy as jnp
from jax import lax
from jax.experimental import pallas as pl
from jax.experimental.pallas import tpu as pltpu
from jax.sharding import Mesh
from jax.sharding import PartitionSpec as P

S = 4
H = 1
CORES = 2

VMEM = pl.BlockSpec(memory_space=pltpu.VMEM)
HBM = pl.BlockSpec(memory_space=pltpu.HBM)
SMEM = pl.BlockSpec(memory_space=pltpu.SMEM)


def start_kernel(*refs):
    half = len(refs) // 2
    sems = refs[-1]
    copies = [pltpu.make_async_copy(a, b, sems.at[i]) for i, (a, b) in enumerate(zip(refs[:half], refs[half:-1]))]
    for copy in copies:
        copy.start()
    for copy in copies:
        copy.wait()


def inner_kernel(offsets_ref, v_ref, blocks_ref, acc_ref):
    count, kinds = blocks_ref.shape[:2]
    for e in range(count):
        total = None
        for k in range(kinds):
            col = e + offsets_ref[k, 0, e]
            inside = jnp.logical_and(col >= 0, col < count)
            lhs = v_ref[jnp.clip(col, 0, count - 1)]
            lhs = jnp.where(inside, lhs, jnp.zeros_like(lhs))
            part = jnp.dot(lhs, blocks_ref[e, k], preferred_element_type=jnp.float32)
            total = part if total is None else total + part
        acc_ref[e] = total


def edge_product(in_chip, offsets_ref, halo_ref, blocks_ref):
    count, kinds = blocks_ref.shape[:2]
    last = count - 1
    chip, core = lax.axis_index("chip"), lax.axis_index("core")
    upper = core == 0 if in_chip else core == 1
    edge = jnp.where(upper, last, 0)
    there = True if in_chip else jnp.where(core == 0, chip > 0, chip < lax.axis_size("chip") - 1)
    halo = halo_ref[...]
    if len(halo_ref.shape) == 3:
        halo = halo_ref[last - edge] if halo_ref.shape[0] == count else halo_ref[0]
    total = None
    for k in range(kinds):
        used = jnp.logical_and(offsets_ref[k, 0, edge] == jnp.where(upper, H, -H), there)
        lhs = jnp.where(used, halo, jnp.zeros_like(halo))
        part = jnp.dot(lhs, blocks_ref[edge, k], preferred_element_type=jnp.float32)
        total = part if total is None else total + part
    return total


def edge_kernel(in_chip, offsets_ref, halo_ref, blocks_ref, out_ref):
    out_ref[...] = edge_product(in_chip, offsets_ref, halo_ref, blocks_ref)


def next_field(grids, first, donor_ref, fringe_ref, weight_ref, live_ref, acc_ref, chip_ref, side, others):
    count = acc_ref.shape[0]
    core, grid = lax.axis_index("core"), lax.axis_index("grid")
    totals = [acc_ref[e] for e in range(count)]
    chip = chip_ref[...]
    totals[0] = totals[0] + jnp.where(core == 0, side, chip)
    totals[-1] = totals[-1] + jnp.where(core == 0, chip, side)
    for s, other in enumerate(others):
        g = lax.rem(grid + grids - 1 - s, grids)
        for c in range(donor_ref.shape[3]):
            target = jnp.where(c < live_ref[0, 0, g], fringe_ref[0, 0, g, c], -1)
            weight = weight_ref[0, 0, g, c]
            value = other[donor_ref[0, 0, g, c] if first else c].astype(jnp.float32)
            for e in range(count):
                totals[e] = totals[e] + jnp.where(target == e, weight, 0.0) * value
    return totals


def outer_kernel(grids, first, *refs):
    take = lambda refs, m: (refs[:m], refs[m:])
    shared, rest = take(refs, 6)
    asked, rest = take(rest, grids - 1)
    others, rest = take(rest, grids - 1)
    side, rest = take(rest, 3 if first else 1)
    v_ref, side_ref, chip_ref, *sends = rest
    side = edge_product(False, *side) if first else side[0][...]
    totals = next_field(grids, first, *shared, side, others)
    count = len(totals)
    fields = [t.astype(jnp.bfloat16) for t in totals]
    for e in range(count):
        v_ref[e] = fields[e]
    start = lax.axis_index("core") == 0
    near, far = (jnp.where(start, *pair) for pair in ((fields[0], fields[-1]), (fields[-1], fields[0])))
    side_ref[0] = near
    side_ref[1] = far
    chip_ref[...] = far
    row = lax.broadcasted_iota(jnp.int32, asked[0].shape[2:], 0) if asked else None
    for s, send_ref in enumerate(sends):
        wish = jnp.where(row == lax.axis_index("grid"), asked[grids - 2 - s][0, 0], 0)
        wish = jnp.sum(wish.astype(jnp.float32), axis=0, keepdims=True)
        for c in range(send_ref.shape[0]):
            index = jnp.broadcast_to(wish[:, c : c + 1], totals[0].shape)
            picked = totals[0]
            for e in range(1, count):
                picked = jnp.where(index == e, totals[e], picked)
            send_ref[c] = picked.astype(jnp.bfloat16)


def early_gram_kernel(*refs):
    fields, (one_ref, two_ref) = refs[:S], refs[S:]
    count, n = fields[0].shape[:2]
    total = None
    for e in range(count):
        rows = jnp.concatenate([f[e] for f in fields], axis=0)
        part = lax.dot_general(rows, rows, (((1,), (1,)), ((), ())), preferred_element_type=jnp.float32)
        total = part if total is None else total + part
    b = lambda i, j0, j1: total[i * n : (i + 1) * n, j0 * n : j1 * n]
    blank = jnp.zeros((n, n), jnp.float32)
    one_ref[...] = jnp.concatenate([*[blank] * (S + 1), b(3, 0, 3)], axis=1)
    two_ref[...] = jnp.concatenate([b(3, 3, 4), b(2, 0, 3), b(1, 0, 2), b(0, 0, 1), blank], axis=1)


def last_kernel(grids, *refs):
    shared, rest = refs[:6], refs[6:]
    others, rest = rest[: grids - 1], rest[grids - 1 :]
    side_ref, *rest = rest
    fields, (one_ref, two_ref, v_ref, keep_ref, send_ref) = rest[:S], rest[S:]
    n, width = one_ref.shape
    total = None
    for e, values in enumerate(next_field(grids, False, *shared, side_ref[...], others)):
        power = values.astype(jnp.bfloat16)
        v_ref[e] = power
        blank = jnp.zeros((width - (S + 1) * n, power.shape[1]), power.dtype)
        rows = jnp.concatenate([*[f[e] for f in fields], power, blank], axis=0)
        part = lax.dot_general(power, rows, (((1,), (1,)), ((), ())), preferred_element_type=jnp.float32)
        total = part if total is None else total + part
    one, two = total + one_ref[...], two_ref[...]
    first = lax.axis_index("core") == 0
    keep_ref[...] = jnp.where(first, one, two)
    send_ref[...] = jnp.where(first, two, one)


def cholesky_rows(panels, height, r_ref):
    size = len(panels) * height
    count = len(panels)
    lane = lax.broadcasted_iota(jnp.int32, (height, size), 1)
    sub = lax.broadcasted_iota(jnp.int32, (height, size), 0)
    panels = list(panels)
    row = lambda x, c: jnp.broadcast_to(x[c : c + 1], (height, size))
    wide = lambda p, j: jnp.broadcast_to(panels[p][:, j : j + 1], (height, size))
    ahead = {c: wide(0, c) for c in range(height)}
    for q in range(count):
        base = q * height
        more = 2 * height if q + 1 < count else height
        side = {(c, p): wide(p, base + c) for c in range(height) for p in range(q + 1, count)}
        side.update({(c, q): ahead[c] for c in range(height)})
        if q + 1 < count:
            side.update({(c, p): wide(p, base + c) for c in range(height, more) for p in (q, q + 1)})
        out = jnp.zeros((height, size), jnp.float32)
        for c in range(height):
            one = row(panels[q], c)
            a = row(side[c, q], c)
            inv = 1.0 / a
            out = jnp.where(sub == c, one * lax.rsqrt(a), out)
            if c + 1 == height and q + 1 == count:
                break
            tops = {e: row(side[e, q], c) for e in range(c + 1, more)}
            scaled = one * inv
            for p in range(q, count):
                if p == q and c + 1 == height:
                    continue
                x = side[c, p] * inv
                panels[p] = panels[p] - x * one
                for e in range(c + 1, more):
                    if (e, p) in side:
                        side[e, p] = side[e, p] - x * tops[e]
        ahead = {c: side[height + c, q + 1] for c in range(height)} if q + 1 < count else {}
        r_ref[base : base + height, :] = jnp.where(lane >= sub + base, out, 0.0)


def factor_kernel(scale, mine_ref, other_ref, r_ref):
    first = lax.axis_index("core") == 0
    mine, other = mine_ref[...] * scale, other_ref[...] * scale
    one, two = jnp.where(first, mine, other), jnp.where(first, other, mine)
    n = one.shape[0]
    size = (S + 1) * n
    b = lambda x, j0, j1: x[:, j0 * n : j1 * n]
    wide = lambda x: jnp.concatenate([x, jnp.zeros((n, size - x.shape[1]), jnp.float32)], axis=1)
    low = jnp.concatenate([
        wide(b(two, 6, 7)),
        wide(b(two, 4, 6)),
        wide(b(two, 1, 4)),
        wide(jnp.concatenate([b(one, 5, 8), b(two, 0, 1)], axis=1)),
        b(one, 0, 5),
    ], axis=0)
    row = lax.broadcasted_iota(jnp.int32, (size, size), 0)
    col = lax.broadcasted_iota(jnp.int32, (size, size), 1)
    a = jnp.where(row >= col, low, low.T)
    height = 8
    cholesky_rows([a[i : i + height] for i in range(0, size, height)], height, r_ref)


def local(rhs, blocks, offsets, donor_elem, fringe_elem, donor_weight, fringe_count):
    _, elem_count, n, unknowns = rhs.shape
    chips, cores, grids = (lax.axis_size(a) for a in ("chip", "core", "grid"))
    axes = ("chip", "core", "grid")
    at = lambda chip, core, grid: (chip * cores + core) * grids + grid % grids
    side = []
    for g in range(grids):
        for chip in range(chips - 1):
            side += [(at(chip, 1, g), at(chip + 1, 0, g)), (at(chip + 1, 0, g), at(chip, 1, g))]
        side += [(at(0, 0, g), at(0, 0, g + 1)), (at(chips - 1, 1, g), at(chips - 1, 1, g + 1))]
    swap = [(0, 1), (1, 0)]

    around = [[(g, (g + s) % grids) for g in range(grids)] for s in range(1, grids)]

    def exchange(to_side, to_chip, *to_grids):
        from_side = lax.ppermute(to_side, axes, side)
        others = [lax.ppermute(v, "grid", pairs) for v, pairs in zip(to_grids, around)]
        return from_side, lax.ppermute(to_chip, "core", swap), others

    slots = donor_elem.shape[3]
    halo_type = jax.ShapeDtypeStruct((n, unknowns), jnp.bfloat16)
    side_type = jax.ShapeDtypeStruct((2, n, unknowns), jnp.bfloat16)
    donor_type = jax.ShapeDtypeStruct((slots, n, unknowns), jnp.bfloat16)
    field_type = jax.ShapeDtypeStruct((elem_count, n, unknowns), jnp.bfloat16)
    edge_type = jax.ShapeDtypeStruct((n, unknowns), jnp.float32)
    acc_type = jax.ShapeDtypeStruct((elem_count, n, unknowns), jnp.float32)
    half_type = jax.ShapeDtypeStruct((n, 8 * n), jnp.float32)
    limit = pltpu.CompilerParams(vmem_limit_bytes=24 << 20)
    rhs, blocks = rhs[0], blocks[0]
    flops = 2 * blocks.size * n
    cost = pl.CostEstimate(flops=flops, bytes_accessed=blocks.size * 2, transcendentals=0)
    edge_cost = pl.CostEstimate(flops=flops // elem_count, bytes_accessed=blocks.size * 2 // elem_count, transcendentals=0)

    small = (jnp.transpose(offsets, (2, 0, 1)), donor_elem, fringe_elem, donor_weight, fringe_count)
    messages = exchange(rhs, rhs, *[rhs] * (grids - 1))
    asked = [lax.ppermute(donor_elem, "grid", pairs) for pairs in around]
    field, offset, *small = pl.pallas_call(
        start_kernel,
        out_shape=(field_type, *(pltpu.SMEM(x.shape, x.dtype) for x in small)),
        in_specs=[HBM] * 6, out_specs=(VMEM, *[SMEM] * 5),
        scratch_shapes=[pltpu.SemaphoreType.DMA((6,))],
        compiler_params=limit, name="start",
        cost_estimate=pl.CostEstimate(flops=2 * 10**9, bytes_accessed=10**6, transcendentals=0),
    )(*(pltpu.with_memory_space_constraint(x, pltpu.HBM) for x in (rhs, *small)))
    basis = [field]
    for level in range(S):
        from_side, from_chip, others = messages
        acc = pl.pallas_call(
            inner_kernel, out_shape=acc_type, in_specs=[SMEM, VMEM, VMEM], out_specs=VMEM,
            compiler_params=limit, name="inner", cost_estimate=cost,
        )(offset, field, blocks)
        edge = lambda in_chip, halo: pl.pallas_call(
            functools.partial(edge_kernel, in_chip), out_shape=edge_type, in_specs=[SMEM, VMEM, VMEM], out_specs=VMEM,
            compiler_params=limit, name="chip_edge" if in_chip else "side_edge", cost_estimate=edge_cost,
        )(offset, halo, blocks)
        shared = (*small, acc, edge(True, from_chip))
        side_in = (offset, from_side, blocks) if level == 0 else (edge(False, from_side),)
        if level + 1 < S:
            field, *sends = pl.pallas_call(
                functools.partial(outer_kernel, grids, level == 0),
                out_shape=(field_type, side_type, halo_type, *[donor_type] * (grids - 1)),
                in_specs=[SMEM] * 4 + [VMEM] * (2 + 2 * (grids - 1)) + ([SMEM] if level == 0 else []) + [VMEM] * len(side_in[-2:]),
                out_specs=(VMEM,) * (3 + grids - 1),
                compiler_params=limit, name="outer",
            )(*shared, *asked, *others, *side_in)
            messages = exchange(*sends)
        else:
            early = pl.pallas_call(
                early_gram_kernel, out_shape=(half_type, half_type),
                in_specs=[VMEM] * S, out_specs=(VMEM, VMEM), compiler_params=limit, name="early_gram", cost_estimate=cost,
            )(*basis)
            field, keep, send = pl.pallas_call(
                functools.partial(last_kernel, grids), out_shape=(field_type, half_type, half_type),
                in_specs=[SMEM] * 4 + [VMEM] * (3 + grids - 1 + S + 2), out_specs=(VMEM,) * 3,
                compiler_params=limit, name="last",
            )(*shared, *others, *side_in, *basis, *early)
        basis.append(field)
    half = keep + lax.ppermute(send, "core", swap)
    parts = lax.all_to_all(jnp.broadcast_to(half[None], (chips * grids, n, 8 * n)), ("chip", "grid"), 0, 0, tiled=True)
    mine = parts.sum(axis=0)
    other = lax.ppermute(mine, "core", swap)
    columns = (S + 1) * n
    row_total = grids * chips * cores * elem_count * unknowns
    r_factor = pl.pallas_call(
        functools.partial(factor_kernel, 1.0 / row_total),
        out_shape=jax.ShapeDtypeStruct((columns, columns), jnp.float32),
        in_specs=[VMEM] * 2, out_specs=VMEM,
        compiler_params=limit, name="factor",
    )(mine, other)
    powers = jnp.stack(basis[1:], axis=1)[None]
    return (powers, r_factor)


def solution(mesh):
    dom, grids = mesh.shape["dom"], mesh.shape["grid"]
    split = Mesh(mesh.devices.reshape(dom // CORES, CORES, grids), ("chip", "core", "grid"))
    where = ("chip", "core")
    in_specs = (
        P("grid", where, None, None),
        P("grid", where, None, None, None),
        P("grid", where, None),
        P("grid", where, None, None),
        P("grid", where, None, None),
        P("grid", where, None, None),
        P("grid", where, None),
    )
    out_specs = (P("grid", where, None, None, None), P())
    return jax.shard_map(local, mesh=split, in_specs=in_specs, out_specs=out_specs, check_vma=False)
```

```python
import functools
import math

import jax
import jax.numpy as jnp
from jax import lax
from jax.experimental import pallas as pl
from jax.experimental.pallas import tpu as pltpu
from jax.sharding import Mesh
from jax.sharding import PartitionSpec as P

S = 4
H = 1
CORES = 2

VMEM = pl.BlockSpec(memory_space=pltpu.VMEM)
HBM = pl.BlockSpec(memory_space=pltpu.HBM)
SMEM = pl.BlockSpec(memory_space=pltpu.SMEM)


def start_kernel(*refs):
    half = len(refs) // 2
    sems = refs[-1]
    copies = [pltpu.make_async_copy(a, b, sems.at[i]) for i, (a, b) in enumerate(zip(refs[:half], refs[half:-1]))]
    for copy in copies:
        copy.start()
    for copy in copies:
        copy.wait()


def inner_kernel(offsets_ref, v_ref, blocks_ref, acc_ref):
    count, kinds = blocks_ref.shape[:2]
    for e in range(count):
        total = None
        for k in range(kinds):
            col = e + offsets_ref[k, 0, e]
            inside = jnp.logical_and(col >= 0, col < count)
            lhs = v_ref[jnp.clip(col, 0, count - 1)]
            lhs = jnp.where(inside, lhs, jnp.zeros_like(lhs))
            part = jnp.dot(lhs, blocks_ref[e, k], preferred_element_type=jnp.float32)
            total = part if total is None else total + part
        acc_ref[e] = total


def edge_product(in_chip, offsets_ref, halo_ref, blocks_ref):
    count, kinds = blocks_ref.shape[:2]
    last = count - 1
    chip, core = lax.axis_index("chip"), lax.axis_index("core")
    upper = core == 0 if in_chip else core == 1
    edge = jnp.where(upper, last, 0)
    there = True if in_chip else jnp.where(core == 0, chip > 0, chip < lax.axis_size("chip") - 1)
    halo = halo_ref[...]
    if len(halo_ref.shape) == 3:
        halo = halo_ref[last - edge] if halo_ref.shape[0] == count else halo_ref[0]
    total = None
    for k in range(kinds):
        used = jnp.logical_and(offsets_ref[k, 0, edge] == jnp.where(upper, H, -H), there)
        lhs = jnp.where(used, halo, jnp.zeros_like(halo))
        part = jnp.dot(lhs, blocks_ref[edge, k], preferred_element_type=jnp.float32)
        total = part if total is None else total + part
    return total


def edge_kernel(in_chip, offsets_ref, halo_ref, blocks_ref, out_ref):
    out_ref[...] = edge_product(in_chip, offsets_ref, halo_ref, blocks_ref)


def next_field(grids, first, donor_ref, fringe_ref, weight_ref, live_ref, acc_ref, chip_ref, side, others):
    count = acc_ref.shape[0]
    core, grid = lax.axis_index("core"), lax.axis_index("grid")
    totals = [acc_ref[e] for e in range(count)]
    chip = chip_ref[...]
    totals[0] = totals[0] + jnp.where(core == 0, side, chip)
    totals[-1] = totals[-1] + jnp.where(core == 0, chip, side)
    for s, other in enumerate(others):
        g = lax.rem(grid + grids - 1 - s, grids)
        for c in range(donor_ref.shape[3]):
            target = jnp.where(c < live_ref[0, 0, g], fringe_ref[0, 0, g, c], -1)
            weight = weight_ref[0, 0, g, c]
            value = other[donor_ref[0, 0, g, c] if first else c].astype(jnp.float32)
            for e in range(count):
                totals[e] = totals[e] + jnp.where(target == e, weight, 0.0) * value
    return totals


def outer_kernel(grids, first, *refs):
    take = lambda refs, m: (refs[:m], refs[m:])
    shared, rest = take(refs, 6)
    asked, rest = take(rest, grids - 1)
    others, rest = take(rest, grids - 1)
    side, rest = take(rest, 3 if first else 1)
    v_ref, side_ref, chip_ref, *sends = rest
    side = edge_product(False, *side) if first else side[0][...]
    totals = next_field(grids, first, *shared, side, others)
    count = len(totals)
    fields = [t.astype(jnp.bfloat16) for t in totals]
    for e in range(count):
        v_ref[e] = fields[e]
    start = lax.axis_index("core") == 0
    near, far = (jnp.where(start, *pair) for pair in ((fields[0], fields[-1]), (fields[-1], fields[0])))
    side_ref[0] = near
    side_ref[1] = far
    chip_ref[...] = far
    row = lax.broadcasted_iota(jnp.int32, asked[0].shape[2:], 0) if asked else None
    for s, send_ref in enumerate(sends):
        wish = jnp.where(row == lax.axis_index("grid"), asked[grids - 2 - s][0, 0], 0)
        wish = jnp.sum(wish.astype(jnp.float32), axis=0, keepdims=True)
        for c in range(send_ref.shape[0]):
            index = jnp.broadcast_to(wish[:, c : c + 1], totals[0].shape)
            picked = totals[0]
            for e in range(1, count):
                picked = jnp.where(index == e, totals[e], picked)
            send_ref[c] = picked.astype(jnp.bfloat16)


def early_gram_kernel(*refs):
    fields, (one_ref, two_ref) = refs[:S], refs[S:]
    count, n = fields[0].shape[:2]
    total = None
    for e in range(count):
        rows = jnp.concatenate([f[e] for f in fields], axis=0)
        part = lax.dot_general(rows, rows, (((1,), (1,)), ((), ())), preferred_element_type=jnp.float32)
        total = part if total is None else total + part
    b = lambda i, j0, j1: total[i * n : (i + 1) * n, j0 * n : j1 * n]
    blank = jnp.zeros((n, n), jnp.float32)
    one_ref[...] = jnp.concatenate([*[blank] * (S + 1), b(3, 0, 3)], axis=1)
    two_ref[...] = jnp.concatenate([b(3, 3, 4), b(2, 0, 3), b(1, 0, 2), b(0, 0, 1), blank], axis=1)


def last_kernel(grids, *refs):
    shared, rest = refs[:6], refs[6:]
    others, rest = rest[: grids - 1], rest[grids - 1 :]
    side_ref, *rest = rest
    fields, (one_ref, two_ref, v_ref, part_ref) = rest[:S], rest[S:]
    n, width = one_ref.shape
    total = None
    for e, values in enumerate(next_field(grids, False, *shared, side_ref[...], others)):
        power = values.astype(jnp.bfloat16)
        v_ref[e] = power
        blank = jnp.zeros((width - (S + 1) * n, power.shape[1]), power.dtype)
        rows = jnp.concatenate([*[f[e] for f in fields], power, blank], axis=0)
        part = lax.dot_general(power, rows, (((1,), (1,)), ((), ())), preferred_element_type=jnp.float32)
        total = part if total is None else total + part
    part_ref[0] = total + one_ref[...]
    part_ref[1] = two_ref[...]


def cholesky_rows(panels, height, r_ref):
    size = len(panels) * height
    count = len(panels)
    lane = lax.broadcasted_iota(jnp.int32, (height, size), 1)
    sub = lax.broadcasted_iota(jnp.int32, (height, size), 0)
    panels = list(panels)
    row = lambda x, c: jnp.broadcast_to(x[c : c + 1], (height, size))
    wide = lambda p, j: jnp.broadcast_to(panels[p][:, j : j + 1], (height, size))
    ahead = {c: wide(0, c) for c in range(height)}
    for q in range(count):
        base = q * height
        more = 2 * height if q + 1 < count else height
        side = {(c, p): wide(p, base + c) for c in range(height) for p in range(q + 1, count)}
        side.update({(c, q): ahead[c] for c in range(height)})
        if q + 1 < count:
            side.update({(c, p): wide(p, base + c) for c in range(height, more) for p in (q, q + 1)})
        out = jnp.zeros((height, size), jnp.float32)
        for c in range(height):
            one = row(panels[q], c)
            a = row(side[c, q], c)
            inv = 1.0 / a
            out = jnp.where(sub == c, one * lax.rsqrt(a), out)
            if c + 1 == height and q + 1 == count:
                break
            tops = {e: row(side[e, q], c) for e in range(c + 1, more)}
            scaled = one * inv
            for p in range(q, count):
                if p == q and c + 1 == height:
                    continue
                x = side[c, p] * inv
                panels[p] = panels[p] - x * one
                for e in range(c + 1, more):
                    if (e, p) in side:
                        side[e, p] = side[e, p] - x * tops[e]
        ahead = {c: side[height + c, q + 1] for c in range(height)} if q + 1 < count else {}
        r_ref[base : base + height, :] = jnp.where(lane >= sub + base, out, 0.0)


def factor_kernel(scale, gram_ref, r_ref):
    one, two = gram_ref[0] * scale, gram_ref[1] * scale
    n = one.shape[0]
    size = (S + 1) * n
    b = lambda x, j0, j1: x[:, j0 * n : j1 * n]
    wide = lambda x: jnp.concatenate([x, jnp.zeros((n, size - x.shape[1]), jnp.float32)], axis=1)
    low = jnp.concatenate([
        wide(b(two, 6, 7)),
        wide(b(two, 4, 6)),
        wide(b(two, 1, 4)),
        wide(jnp.concatenate([b(one, 5, 8), b(two, 0, 1)], axis=1)),
        b(one, 0, 5),
    ], axis=0)
    row = lax.broadcasted_iota(jnp.int32, (size, size), 0)
    col = lax.broadcasted_iota(jnp.int32, (size, size), 1)
    a = jnp.where(row >= col, low, low.T)
    height = 8
    cholesky_rows([a[i : i + height] for i in range(0, size, height)], height, r_ref)


def primes(value):
    found, p = [], 2
    while value > 1:
        while value % p == 0:
            found.append(p)
            value //= p
        p += 1
    return found


def sum_stages(chips, grids):
    digits, step = [], 1
    for size in primes(chips):
        digits.append((0, step, size))
        step *= size
    step, places = 1, []
    for size in primes(grids):
        places.append((1, step, size))
        step *= size
    digits[1:1] = places

    def moved(place, digit, by):
        axis, step, size = digit
        now = place[axis] // step % size
        place[axis] += ((now + by) % size - now) * step

    stages = []
    for i in range(0, len(digits), 2):
        pair, group = digits[i : i + 2], []
        for shift in range(1, math.prod(d[2] for d in pair)):
            pairs = []
            for chip in range(chips):
                for core in range(CORES):
                    for grid in range(grids):
                        place = [chip, grid]
                        moved(place, pair[0], shift % pair[0][2])
                        moved(place, pair[-1], shift // pair[0][2])
                        pairs.append(((chip * CORES + core) * grids + grid, (place[0] * CORES + 1 - core) * grids + place[1]))
            group.append(pairs)
        stages.append(group)
    return stages


def local(rhs, blocks, offsets, donor_elem, fringe_elem, donor_weight, fringe_count):
    _, elem_count, n, unknowns = rhs.shape
    chips, cores, grids = (lax.axis_size(a) for a in ("chip", "core", "grid"))
    axes = ("chip", "core", "grid")
    at = lambda chip, core, grid: (chip * cores + core) * grids + grid % grids
    side = []
    for g in range(grids):
        for chip in range(chips - 1):
            side += [(at(chip, 1, g), at(chip + 1, 0, g)), (at(chip + 1, 0, g), at(chip, 1, g))]
        side += [(at(0, 0, g), at(0, 0, g + 1)), (at(chips - 1, 1, g), at(chips - 1, 1, g + 1))]
    swap = [(0, 1), (1, 0)]

    around = [[(g, (g + s) % grids) for g in range(grids)] for s in range(1, grids)]

    def exchange(to_side, to_chip, *to_grids):
        from_side = lax.ppermute(to_side, axes, side)
        others = [lax.ppermute(v, "grid", pairs) for v, pairs in zip(to_grids, around)]
        return from_side, lax.ppermute(to_chip, "core", swap), others

    slots = donor_elem.shape[3]
    halo_type = jax.ShapeDtypeStruct((n, unknowns), jnp.bfloat16)
    side_type = jax.ShapeDtypeStruct((2, n, unknowns), jnp.bfloat16)
    donor_type = jax.ShapeDtypeStruct((slots, n, unknowns), jnp.bfloat16)
    field_type = jax.ShapeDtypeStruct((elem_count, n, unknowns), jnp.bfloat16)
    edge_type = jax.ShapeDtypeStruct((n, unknowns), jnp.float32)
    acc_type = jax.ShapeDtypeStruct((elem_count, n, unknowns), jnp.float32)
    half_type = jax.ShapeDtypeStruct((n, 8 * n), jnp.float32)
    gram_type = jax.ShapeDtypeStruct((2, n, 8 * n), jnp.float32)
    limit = pltpu.CompilerParams(vmem_limit_bytes=24 << 20)
    rhs, blocks = rhs[0], blocks[0]
    flops = 2 * blocks.size * n
    cost = pl.CostEstimate(flops=flops, bytes_accessed=blocks.size * 2, transcendentals=0)
    edge_cost = pl.CostEstimate(flops=flops // elem_count, bytes_accessed=blocks.size * 2 // elem_count, transcendentals=0)

    small = (jnp.transpose(offsets, (2, 0, 1)), donor_elem, fringe_elem, donor_weight, fringe_count)
    messages = exchange(rhs, rhs, *[rhs] * (grids - 1))
    asked = [lax.ppermute(donor_elem, "grid", pairs) for pairs in around]
    field, offset, *small = pl.pallas_call(
        start_kernel,
        out_shape=(field_type, *(pltpu.SMEM(x.shape, x.dtype) for x in small)),
        in_specs=[HBM] * 6, out_specs=(VMEM, *[SMEM] * 5),
        scratch_shapes=[pltpu.SemaphoreType.DMA((6,))],
        compiler_params=limit, name="start",
        cost_estimate=pl.CostEstimate(flops=2 * 10**9, bytes_accessed=10**6, transcendentals=0),
    )(*(pltpu.with_memory_space_constraint(x, pltpu.HBM) for x in (rhs, *small)))
    basis = [field]
    for level in range(S):
        from_side, from_chip, others = messages
        acc = pl.pallas_call(
            inner_kernel, out_shape=acc_type, in_specs=[SMEM, VMEM, VMEM], out_specs=VMEM,
            compiler_params=limit, name="inner", cost_estimate=cost,
        )(offset, field, blocks)
        edge = lambda in_chip, halo: pl.pallas_call(
            functools.partial(edge_kernel, in_chip), out_shape=edge_type, in_specs=[SMEM, VMEM, VMEM], out_specs=VMEM,
            compiler_params=limit, name="chip_edge" if in_chip else "side_edge", cost_estimate=edge_cost,
        )(offset, halo, blocks)
        shared = (*small, acc, edge(True, from_chip))
        side_in = (offset, from_side, blocks) if level == 0 else (edge(False, from_side),)
        if level + 1 < S:
            field, *sends = pl.pallas_call(
                functools.partial(outer_kernel, grids, level == 0),
                out_shape=(field_type, side_type, halo_type, *[donor_type] * (grids - 1)),
                in_specs=[SMEM] * 4 + [VMEM] * (2 + 2 * (grids - 1)) + ([SMEM] if level == 0 else []) + [VMEM] * len(side_in[-2:]),
                out_specs=(VMEM,) * (3 + grids - 1),
                compiler_params=limit, name="outer",
            )(*shared, *asked, *others, *side_in)
            messages = exchange(*sends)
        else:
            early = pl.pallas_call(
                early_gram_kernel, out_shape=(half_type, half_type),
                in_specs=[VMEM] * S, out_specs=(VMEM, VMEM), compiler_params=limit, name="early_gram", cost_estimate=cost,
            )(*basis)
            field, gram = pl.pallas_call(
                functools.partial(last_kernel, grids), out_shape=(field_type, gram_type),
                in_specs=[SMEM] * 4 + [VMEM] * (3 + grids - 1 + S + 2), out_specs=(VMEM,) * 2,
                compiler_params=limit, name="last",
            )(*shared, *others, *side_in, *basis, *early)
        basis.append(field)
    gram = gram + lax.ppermute(gram, "core", swap)
    for group in sum_stages(chips, grids):
        arrived = [lax.ppermute(gram, axes, pairs) for pairs in group]
        for part in arrived:
            gram = gram + part
    columns = (S + 1) * n
    row_total = grids * chips * cores * elem_count * unknowns
    r_factor = pl.pallas_call(
        functools.partial(factor_kernel, 1.0 / row_total),
        out_shape=jax.ShapeDtypeStruct((columns, columns), jnp.float32),
        in_specs=[VMEM], out_specs=VMEM,
        compiler_params=limit, name="factor",
    )(gram)
    powers = jnp.stack(basis[1:], axis=1)[None]
    return (powers, r_factor)


def solution(mesh):
    dom, grids = mesh.shape["dom"], mesh.shape["grid"]
    split = Mesh(mesh.devices.reshape(dom // CORES, CORES, grids), ("chip", "core", "grid"))
    where = ("chip", "core")
    in_specs = (
        P("grid", where, None, None),
        P("grid", where, None, None, None),
        P("grid", where, None),
        P("grid", where, None, None),
        P("grid", where, None, None),
        P("grid", where, None, None),
        P("grid", where, None),
    )
    out_specs = (P("grid", where, None, None, None), P())
    return jax.shard_map(local, mesh=split, in_specs=in_specs, out_specs=out_specs, check_vma=False)
```

```python
import functools
import math

import jax
import jax.numpy as jnp
from jax import lax
from jax.experimental import pallas as pl
from jax.experimental.pallas import tpu as pltpu
from jax.sharding import Mesh
from jax.sharding import PartitionSpec as P

S = 4
H = 1
CORES = 2

VMEM = pl.BlockSpec(memory_space=pltpu.VMEM)
HBM = pl.BlockSpec(memory_space=pltpu.HBM)
SMEM = pl.BlockSpec(memory_space=pltpu.SMEM)


def start_kernel(*refs):
    half = len(refs) // 2
    sems = refs[-1]
    copies = [pltpu.make_async_copy(a, b, sems.at[i]) for i, (a, b) in enumerate(zip(refs[:half], refs[half:-1]))]
    for copy in copies:
        copy.start()
    for copy in copies:
        copy.wait()


def inner_kernel(offsets_ref, v_ref, blocks_ref, acc_ref):
    count, kinds = blocks_ref.shape[:2]
    for e in range(count):
        total = None
        for k in range(kinds):
            col = e + offsets_ref[k, 0, e]
            inside = jnp.logical_and(col >= 0, col < count)
            lhs = v_ref[jnp.clip(col, 0, count - 1)]
            lhs = jnp.where(inside, lhs, jnp.zeros_like(lhs))
            part = jnp.dot(lhs, blocks_ref[e, k], preferred_element_type=jnp.float32)
            total = part if total is None else total + part
        acc_ref[e] = total


def edge_place(in_chip, count, halo_ref):
    last = count - 1
    chip, core = lax.axis_index("chip"), lax.axis_index("core")
    upper = core == 0 if in_chip else core == 1
    edge = jnp.where(upper, last, 0)
    there = True if in_chip else jnp.where(core == 0, chip > 0, chip < lax.axis_size("chip") - 1)
    if len(halo_ref.shape) == 2:
        return upper, edge, there, halo_ref[...]
    return upper, edge, there, halo_ref[last - edge] if halo_ref.shape[0] == count else halo_ref[0]


def edge_product(in_chip, offsets_ref, halo_ref, blocks_ref):
    count, kinds = blocks_ref.shape[:2]
    upper, edge, there, halo = edge_place(in_chip, count, halo_ref)
    total = None
    for k in range(kinds):
        used = jnp.logical_and(offsets_ref[k, 0, edge] == jnp.where(upper, H, -H), there)
        lhs = jnp.where(used, halo, jnp.zeros_like(halo))
        part = jnp.dot(lhs, blocks_ref[edge, k], preferred_element_type=jnp.float32)
        total = part if total is None else total + part
    return total


def edge_kernel(in_chip, offsets_ref, halo_ref, blocks_ref, out_ref):
    count, kinds = blocks_ref.shape[:2]
    upper, edge, there, halo = edge_place(in_chip, count, halo_ref)
    hits = [jnp.logical_and(offsets_ref[k, 0, edge] == jnp.where(upper, H, -H), there) for k in range(kinds)]
    number = sum(hit.astype(jnp.int32) for hit in hits)
    first = jnp.int32(kinds - 1)
    for k in range(kinds - 2, -1, -1):
        first = jnp.where(hits[k], k, first)

    @pl.when(number <= 1)
    def _():
        lhs = jnp.where(number > 0, halo, jnp.zeros_like(halo))
        out_ref[...] = jnp.dot(lhs, blocks_ref[edge, first], preferred_element_type=jnp.float32)

    @pl.when(number > 1)
    def _():
        out_ref[...] = edge_product(in_chip, offsets_ref, halo_ref, blocks_ref)


def next_field(grids, first, donor_ref, fringe_ref, weight_ref, live_ref, acc_ref, chip_ref, side, others):
    count = acc_ref.shape[0]
    core, grid = lax.axis_index("core"), lax.axis_index("grid")
    totals = [acc_ref[e] for e in range(count)]
    chip = chip_ref[...]
    totals[0] = totals[0] + jnp.where(core == 0, side, chip)
    totals[-1] = totals[-1] + jnp.where(core == 0, chip, side)
    for s, other in enumerate(others):
        g = lax.rem(grid + grids - 1 - s, grids)
        for c in range(donor_ref.shape[3]):
            target = jnp.where(c < live_ref[0, 0, g], fringe_ref[0, 0, g, c], -1)
            weight = weight_ref[0, 0, g, c]
            value = other[donor_ref[0, 0, g, c] if first else c].astype(jnp.float32)
            for e in range(count):
                totals[e] = totals[e] + jnp.where(target == e, weight, 0.0) * value
    return totals


def outer_kernel(grids, first, *refs):
    take = lambda refs, m: (refs[:m], refs[m:])
    shared, rest = take(refs, 6)
    asked, rest = take(rest, grids - 1)
    others, rest = take(rest, grids - 1)
    side, rest = take(rest, 3 if first else 1)
    v_ref, side_ref, chip_ref, *sends, edge_ref = rest if first else (*rest, None)
    if first:
        edge_kernel(False, *side, edge_ref)
    side = edge_ref[...] if first else side[0][...]
    totals = next_field(grids, first, *shared, side, others)
    count = len(totals)
    fields = [t.astype(jnp.bfloat16) for t in totals]
    for e in range(count):
        v_ref[e] = fields[e]
    start = lax.axis_index("core") == 0
    near, far = (jnp.where(start, *pair) for pair in ((fields[0], fields[-1]), (fields[-1], fields[0])))
    side_ref[0] = near
    side_ref[1] = far
    chip_ref[...] = far
    row = lax.broadcasted_iota(jnp.int32, asked[0].shape[2:], 0) if asked else None
    for s, send_ref in enumerate(sends):
        wish = jnp.where(row == lax.axis_index("grid"), asked[grids - 2 - s][0, 0], 0)
        wish = jnp.sum(wish.astype(jnp.float32), axis=0, keepdims=True)
        for c in range(send_ref.shape[0]):
            index = jnp.broadcast_to(wish[:, c : c + 1], totals[0].shape)
            picked = totals[0]
            for e in range(1, count):
                picked = jnp.where(index == e, totals[e], picked)
            send_ref[c] = picked.astype(jnp.bfloat16)


def early_gram_kernel(*refs):
    fields, (one_ref, two_ref) = refs[:S], refs[S:]
    count, n = fields[0].shape[:2]
    total = None
    for e in range(count):
        rows = jnp.concatenate([f[e] for f in fields], axis=0)
        part = lax.dot_general(rows, rows, (((1,), (1,)), ((), ())), preferred_element_type=jnp.float32)
        total = part if total is None else total + part
    b = lambda i, j0, j1: total[i * n : (i + 1) * n, j0 * n : j1 * n]
    blank = jnp.zeros((n, n), jnp.float32)
    one_ref[...] = jnp.concatenate([*[blank] * (S + 1), b(3, 0, 3)], axis=1)
    two_ref[...] = jnp.concatenate([b(3, 3, 4), b(2, 0, 3), b(1, 0, 2), b(0, 0, 1), blank], axis=1)


def last_kernel(grids, *refs):
    shared, rest = refs[:6], refs[6:]
    others, rest = rest[: grids - 1], rest[grids - 1 :]
    side_ref, *rest = rest
    fields, (one_ref, two_ref, v_ref, part_ref) = rest[:S], rest[S:]
    n, width = one_ref.shape
    total = None
    for e, values in enumerate(next_field(grids, False, *shared, side_ref[...], others)):
        power = values.astype(jnp.bfloat16)
        v_ref[e] = power
        blank = jnp.zeros((width - (S + 1) * n, power.shape[1]), power.dtype)
        rows = jnp.concatenate([*[f[e] for f in fields], power, blank], axis=0)
        part = lax.dot_general(power, rows, (((1,), (1,)), ((), ())), preferred_element_type=jnp.float32)
        total = part if total is None else total + part
    part_ref[0] = total + one_ref[...]
    part_ref[1] = two_ref[...]


def cholesky_rows(panels, height, r_ref):
    size = len(panels) * height
    count = len(panels)
    lane = lax.broadcasted_iota(jnp.int32, (height, size), 1)
    sub = lax.broadcasted_iota(jnp.int32, (height, size), 0)
    panels = list(panels)
    row = lambda x, c: jnp.broadcast_to(x[c : c + 1], (height, size))
    wide = lambda p, j: jnp.broadcast_to(panels[p][:, j : j + 1], (height, size))
    ahead = {c: wide(0, c) for c in range(height)}
    for q in range(count):
        base = q * height
        more = 2 * height if q + 1 < count else height
        side = {(c, p): wide(p, base + c) for c in range(height) for p in range(q + 1, count)}
        side.update({(c, q): ahead[c] for c in range(height)})
        if q + 1 < count:
            side.update({(c, p): wide(p, base + c) for c in range(height, more) for p in (q, q + 1)})
        out = jnp.zeros((height, size), jnp.float32)
        for c in range(height):
            one = row(panels[q], c)
            a = row(side[c, q], c)
            inv = 1.0 / a
            out = jnp.where(sub == c, one * lax.rsqrt(a), out)
            if c + 1 == height and q + 1 == count:
                break
            tops = {e: row(side[e, q], c) for e in range(c + 1, more)}
            scaled = one * inv
            for p in range(q, count):
                if p == q and c + 1 == height:
                    continue
                x = side[c, p] * inv
                panels[p] = panels[p] - x * one
                for e in range(c + 1, more):
                    if (e, p) in side:
                        side[e, p] = side[e, p] - x * tops[e]
        ahead = {c: side[height + c, q + 1] for c in range(height)} if q + 1 < count else {}
        r_ref[base : base + height, :] = jnp.where(lane >= sub + base, out, 0.0)


def factor_kernel(scale, gram_ref, r_ref):
    one, two = gram_ref[0] * scale, gram_ref[1] * scale
    n = one.shape[0]
    size = (S + 1) * n
    b = lambda x, j0, j1: x[:, j0 * n : j1 * n]
    wide = lambda x: jnp.concatenate([x, jnp.zeros((n, size - x.shape[1]), jnp.float32)], axis=1)
    low = jnp.concatenate([
        wide(b(two, 6, 7)),
        wide(b(two, 4, 6)),
        wide(b(two, 1, 4)),
        wide(jnp.concatenate([b(one, 5, 8), b(two, 0, 1)], axis=1)),
        b(one, 0, 5),
    ], axis=0)
    row = lax.broadcasted_iota(jnp.int32, (size, size), 0)
    col = lax.broadcasted_iota(jnp.int32, (size, size), 1)
    a = jnp.where(row >= col, low, low.T)
    height = 8
    cholesky_rows([a[i : i + height] for i in range(0, size, height)], height, r_ref)


def primes(value):
    found, p = [], 2
    while value > 1:
        while value % p == 0:
            found.append(p)
            value //= p
        p += 1
    return found


def sum_stages(chips, grids):
    digits, step = [], 1
    for size in primes(chips):
        digits.append((0, step, size))
        step *= size
    step, places = 1, []
    for size in primes(grids):
        places.append((1, step, size))
        step *= size
    digits[1:1] = places

    def moved(place, digit, by):
        axis, step, size = digit
        now = place[axis] // step % size
        place[axis] += ((now + by) % size - now) * step

    stages = []
    for i in range(0, len(digits), 2):
        pair, group = digits[i : i + 2], []
        for shift in range(1, math.prod(d[2] for d in pair)):
            pairs = []
            for chip in range(chips):
                for core in range(CORES):
                    for grid in range(grids):
                        place = [chip, grid]
                        moved(place, pair[0], shift % pair[0][2])
                        moved(place, pair[-1], shift // pair[0][2])
                        pairs.append(((chip * CORES + core) * grids + grid, (place[0] * CORES + 1 - core) * grids + place[1]))
            group.append(pairs)
        stages.append(group)
    return stages


def local(rhs, blocks, offsets, donor_elem, fringe_elem, donor_weight, fringe_count):
    _, elem_count, n, unknowns = rhs.shape
    chips, cores, grids = (lax.axis_size(a) for a in ("chip", "core", "grid"))
    axes = ("chip", "core", "grid")
    at = lambda chip, core, grid: (chip * cores + core) * grids + grid % grids
    side = []
    for g in range(grids):
        for chip in range(chips - 1):
            side += [(at(chip, 1, g), at(chip + 1, 0, g)), (at(chip + 1, 0, g), at(chip, 1, g))]
        side += [(at(0, 0, g), at(0, 0, g + 1)), (at(chips - 1, 1, g), at(chips - 1, 1, g + 1))]
    swap = [(0, 1), (1, 0)]

    around = [[(g, (g + s) % grids) for g in range(grids)] for s in range(1, grids)]

    def exchange(to_side, to_chip, *to_grids):
        from_side = lax.ppermute(to_side, axes, side)
        others = [lax.ppermute(v, "grid", pairs) for v, pairs in zip(to_grids, around)]
        return from_side, lax.ppermute(to_chip, "core", swap), others

    slots = donor_elem.shape[3]
    halo_type = jax.ShapeDtypeStruct((n, unknowns), jnp.bfloat16)
    side_type = jax.ShapeDtypeStruct((2, n, unknowns), jnp.bfloat16)
    donor_type = jax.ShapeDtypeStruct((slots, n, unknowns), jnp.bfloat16)
    field_type = jax.ShapeDtypeStruct((elem_count, n, unknowns), jnp.bfloat16)
    edge_type = jax.ShapeDtypeStruct((n, unknowns), jnp.float32)
    acc_type = jax.ShapeDtypeStruct((elem_count, n, unknowns), jnp.float32)
    half_type = jax.ShapeDtypeStruct((n, 8 * n), jnp.float32)
    gram_type = jax.ShapeDtypeStruct((2, n, 8 * n), jnp.float32)
    limit = pltpu.CompilerParams(vmem_limit_bytes=24 << 20)
    rhs, blocks = rhs[0], blocks[0]
    flops = 2 * blocks.size * n
    cost = pl.CostEstimate(flops=flops, bytes_accessed=blocks.size * 2, transcendentals=0)
    edge_cost = pl.CostEstimate(flops=flops // elem_count, bytes_accessed=blocks.size * 2 // elem_count, transcendentals=0)

    small = (jnp.transpose(offsets, (2, 0, 1)), donor_elem, fringe_elem, donor_weight, fringe_count)
    messages = exchange(rhs, rhs, *[rhs] * (grids - 1))
    asked = [lax.ppermute(donor_elem, "grid", pairs) for pairs in around]
    field, offset, *small = pl.pallas_call(
        start_kernel,
        out_shape=(field_type, *(pltpu.SMEM(x.shape, x.dtype) for x in small)),
        in_specs=[HBM] * 6, out_specs=(VMEM, *[SMEM] * 5),
        scratch_shapes=[pltpu.SemaphoreType.DMA((6,))],
        compiler_params=limit, name="start",
        cost_estimate=pl.CostEstimate(flops=2 * 10**9, bytes_accessed=10**6, transcendentals=0),
    )(*(pltpu.with_memory_space_constraint(x, pltpu.HBM) for x in (rhs, *small)))
    basis = [field]
    for level in range(S):
        from_side, from_chip, others = messages
        acc = pl.pallas_call(
            inner_kernel, out_shape=acc_type, in_specs=[SMEM, VMEM, VMEM], out_specs=VMEM,
            compiler_params=limit, name="inner", cost_estimate=cost,
        )(offset, field, blocks)
        edge = lambda in_chip, halo: pl.pallas_call(
            functools.partial(edge_kernel, in_chip), out_shape=edge_type, in_specs=[SMEM, VMEM, VMEM], out_specs=VMEM,
            compiler_params=limit, name="chip_edge" if in_chip else "side_edge", cost_estimate=edge_cost,
        )(offset, halo, blocks)
        shared = (*small, acc, edge(True, from_chip))
        side_in = (offset, from_side, blocks) if level == 0 else (edge(False, from_side),)
        if level + 1 < S:
            field, *sends = pl.pallas_call(
                functools.partial(outer_kernel, grids, level == 0),
                out_shape=(field_type, side_type, halo_type, *[donor_type] * (grids - 1)),
                in_specs=[SMEM] * 4 + [VMEM] * (2 + 2 * (grids - 1)) + ([SMEM] if level == 0 else []) + [VMEM] * len(side_in[-2:]),
                out_specs=(VMEM,) * (3 + grids - 1),
                scratch_shapes=[pltpu.VMEM((n, unknowns), jnp.float32)] if level == 0 else [],
                compiler_params=limit, name="outer",
            )(*shared, *asked, *others, *side_in)
            messages = exchange(*sends)
        else:
            early = pl.pallas_call(
                early_gram_kernel, out_shape=(half_type, half_type),
                in_specs=[VMEM] * S, out_specs=(VMEM, VMEM), compiler_params=limit, name="early_gram", cost_estimate=cost,
            )(*basis)
            field, gram = pl.pallas_call(
                functools.partial(last_kernel, grids), out_shape=(field_type, gram_type),
                in_specs=[SMEM] * 4 + [VMEM] * (3 + grids - 1 + S + 2), out_specs=(VMEM,) * 2,
                compiler_params=limit, name="last",
            )(*shared, *others, *side_in, *basis, *early)
        basis.append(field)
    gram = gram + lax.ppermute(gram, "core", swap)
    for group in sum_stages(chips, grids):
        arrived = [lax.ppermute(gram, axes, pairs) for pairs in group]
        for part in arrived:
            gram = gram + part
    columns = (S + 1) * n
    row_total = grids * chips * cores * elem_count * unknowns
    r_factor = pl.pallas_call(
        functools.partial(factor_kernel, 1.0 / row_total),
        out_shape=jax.ShapeDtypeStruct((columns, columns), jnp.float32),
        in_specs=[VMEM], out_specs=VMEM,
        compiler_params=limit, name="factor",
    )(gram)
    powers = jnp.stack(basis[1:], axis=1)[None]
    return (powers, r_factor)


def solution(mesh):
    dom, grids = mesh.shape["dom"], mesh.shape["grid"]
    split = Mesh(mesh.devices.reshape(dom // CORES, CORES, grids), ("chip", "core", "grid"))
    where = ("chip", "core")
    in_specs = (
        P("grid", where, None, None),
        P("grid", where, None, None, None),
        P("grid", where, None),
        P("grid", where, None, None),
        P("grid", where, None, None),
        P("grid", where, None, None),
        P("grid", where, None),
    )
    out_specs = (P("grid", where, None, None, None), P())
    return jax.shard_map(local, mesh=split, in_specs=in_specs, out_specs=out_specs, check_vma=False)
```

```python
import functools
import math

import jax
import jax.numpy as jnp
from jax import lax
from jax.experimental import pallas as pl
from jax.experimental.pallas import tpu as pltpu
from jax.sharding import Mesh
from jax.sharding import PartitionSpec as P

S = 4
H = 1
CORES = 2

VMEM = pl.BlockSpec(memory_space=pltpu.VMEM)
HBM = pl.BlockSpec(memory_space=pltpu.HBM)
SMEM = pl.BlockSpec(memory_space=pltpu.SMEM)


def start_kernel(*refs):
    half = len(refs) // 2
    sems = refs[-1]
    copies = [pltpu.make_async_copy(a, b, sems.at[i]) for i, (a, b) in enumerate(zip(refs[:half], refs[half:-1]))]
    for copy in copies:
        copy.start()
    for copy in copies:
        copy.wait()


def inner_kernel(offsets_ref, v_ref, blocks_ref, acc_ref):
    count, kinds = blocks_ref.shape[:2]
    for e in range(count):
        total = None
        for k in range(kinds):
            col = e + offsets_ref[k, 0, e]
            inside = jnp.logical_and(col >= 0, col < count)
            lhs = v_ref[jnp.clip(col, 0, count - 1)]
            lhs = jnp.where(inside, lhs, jnp.zeros_like(lhs))
            part = jnp.dot(lhs, blocks_ref[e, k], preferred_element_type=jnp.float32)
            total = part if total is None else total + part
        acc_ref[e] = total


def edge_place(in_chip, count, halo_ref):
    last = count - 1
    chip, core = lax.axis_index("chip"), lax.axis_index("core")
    upper = core == 0 if in_chip else core == 1
    edge = jnp.where(upper, last, 0)
    there = True if in_chip else jnp.where(core == 0, chip > 0, chip < lax.axis_size("chip") - 1)
    if len(halo_ref.shape) == 2:
        return upper, edge, there, halo_ref[...]
    return upper, edge, there, halo_ref[last - edge] if halo_ref.shape[0] == count else halo_ref[0]


def edge_product(in_chip, offsets_ref, halo_ref, blocks_ref):
    count, kinds = blocks_ref.shape[:2]
    upper, edge, there, halo = edge_place(in_chip, count, halo_ref)
    total = None
    for k in range(kinds):
        used = jnp.logical_and(offsets_ref[k, 0, edge] == jnp.where(upper, H, -H), there)
        lhs = jnp.where(used, halo, jnp.zeros_like(halo))
        part = jnp.dot(lhs, blocks_ref[edge, k], preferred_element_type=jnp.float32)
        total = part if total is None else total + part
    return total


def edge_kernel(in_chip, offsets_ref, halo_ref, blocks_ref, out_ref):
    count, kinds = blocks_ref.shape[:2]
    upper, edge, there, halo = edge_place(in_chip, count, halo_ref)
    hits = [jnp.logical_and(offsets_ref[k, 0, edge] == jnp.where(upper, H, -H), there) for k in range(kinds)]
    number = sum(hit.astype(jnp.int32) for hit in hits)
    first = jnp.int32(kinds - 1)
    for k in range(kinds - 2, -1, -1):
        first = jnp.where(hits[k], k, first)

    @pl.when(number <= 1)
    def _():
        lhs = jnp.where(number > 0, halo, jnp.zeros_like(halo))
        out_ref[...] = jnp.dot(lhs, blocks_ref[edge, first], preferred_element_type=jnp.float32)

    @pl.when(number > 1)
    def _():
        out_ref[...] = edge_product(in_chip, offsets_ref, halo_ref, blocks_ref)


def next_field(grids, first, donor_ref, fringe_ref, weight_ref, live_ref, acc_ref, chip_ref, side, others):
    count = acc_ref.shape[0]
    core, grid = lax.axis_index("core"), lax.axis_index("grid")
    totals = [acc_ref[e] for e in range(count)]
    chip = chip_ref[...]
    totals[0] = totals[0] + jnp.where(core == 0, side, chip)
    totals[-1] = totals[-1] + jnp.where(core == 0, chip, side)
    for s, other in enumerate(others):
        g = lax.rem(grid + grids - 1 - s, grids)
        for c in range(donor_ref.shape[3]):
            target = jnp.where(c < live_ref[0, 0, g], fringe_ref[0, 0, g, c], -1)
            weight = weight_ref[0, 0, g, c]
            value = other[donor_ref[0, 0, g, c] if first else c].astype(jnp.float32)
            for e in range(count):
                totals[e] = totals[e] + jnp.where(target == e, weight, 0.0) * value
    return totals


def outer_kernel(grids, first, *refs):
    take = lambda refs, m: (refs[:m], refs[m:])
    shared, rest = take(refs, 6)
    asked, rest = take(rest, grids - 1)
    others, rest = take(rest, grids - 1)
    side, rest = take(rest, 3 if first else 1)
    v_ref, side_ref, chip_ref, *sends, edge_ref = rest if first else (*rest, None)
    if first:
        edge_kernel(False, *side, edge_ref)
    side = edge_ref[...] if first else side[0][...]
    totals = next_field(grids, first, *shared, side, others)
    count = len(totals)
    fields = [t.astype(jnp.bfloat16) for t in totals]
    for e in range(count):
        v_ref[e] = fields[e]
    start = lax.axis_index("core") == 0
    near, far = (jnp.where(start, *pair) for pair in ((fields[0], fields[-1]), (fields[-1], fields[0])))
    side_ref[0] = near
    side_ref[1] = far
    chip_ref[...] = far
    row = lax.broadcasted_iota(jnp.int32, asked[0].shape[2:], 0) if asked else None
    for s, send_ref in enumerate(sends):
        wish = jnp.where(row == lax.axis_index("grid"), asked[grids - 2 - s][0, 0], 0)
        wish = jnp.sum(wish.astype(jnp.float32), axis=0, keepdims=True)
        for c in range(send_ref.shape[0]):
            index = jnp.broadcast_to(wish[:, c : c + 1], totals[0].shape)
            picked = totals[0]
            for e in range(1, count):
                picked = jnp.where(index == e, totals[e], picked)
            send_ref[c] = picked.astype(jnp.bfloat16)


def early_gram_kernel(*refs):
    fields, (one_ref, two_ref) = refs[:S], refs[S:]
    count, n = fields[0].shape[:2]
    total = None
    for e in range(count):
        rows = jnp.concatenate([f[e] for f in fields], axis=0)
        part = lax.dot_general(rows, rows, (((1,), (1,)), ((), ())), preferred_element_type=jnp.float32)
        total = part if total is None else total + part
    b = lambda i, j0, j1: total[i * n : (i + 1) * n, j0 * n : j1 * n]
    blank = jnp.zeros((n, n), jnp.float32)
    one_ref[...] = jnp.concatenate([*[blank] * (S + 1), b(3, 0, 3)], axis=1)
    two_ref[...] = jnp.concatenate([b(3, 3, 4), b(2, 0, 3), b(1, 0, 2), b(0, 0, 1), blank], axis=1)


def last_kernel(grids, *refs):
    shared, rest = refs[:6], refs[6:]
    others, rest = rest[: grids - 1], rest[grids - 1 :]
    side_ref, *rest = rest
    fields, (one_ref, two_ref, v_ref, part_ref) = rest[:S], rest[S:]
    n, width = one_ref.shape
    total = None
    for e, values in enumerate(next_field(grids, False, *shared, side_ref[...], others)):
        power = values.astype(jnp.bfloat16)
        v_ref[e] = power
        blank = jnp.zeros((width - (S + 1) * n, power.shape[1]), power.dtype)
        rows = jnp.concatenate([*[f[e] for f in fields], power, blank], axis=0)
        part = lax.dot_general(power, rows, (((1,), (1,)), ((), ())), preferred_element_type=jnp.float32)
        total = part if total is None else total + part
    part_ref[0] = total + one_ref[...]
    part_ref[1] = two_ref[...]


def cholesky_rows(panels, height, r_ref):
    size = len(panels) * height
    count = len(panels)
    lane = lax.broadcasted_iota(jnp.int32, (height, size), 1)
    sub = lax.broadcasted_iota(jnp.int32, (height, size), 0)
    panels = list(panels)
    row = lambda x, c: jnp.broadcast_to(x[c : c + 1], (height, size))
    wide = lambda p, j: jnp.broadcast_to(panels[p][:, j : j + 1], (height, size))
    ahead = {c: wide(0, c) for c in range(height)}
    for q in range(count):
        base = q * height
        more = 2 * height if q + 1 < count else height
        side = {(c, p): wide(p, base + c) for c in range(height) for p in range(q + 1, count)}
        side.update({(c, q): ahead[c] for c in range(height)})
        if q + 1 < count:
            side.update({(c, p): wide(p, base + c) for c in range(height, more) for p in (q, q + 1)})
        out = jnp.zeros((height, size), jnp.float32)
        for c in range(height):
            one = row(panels[q], c)
            a = row(side[c, q], c)
            inv = 1.0 / a
            out = jnp.where(sub == c, one * lax.rsqrt(a), out)
            if c + 1 == height and q + 1 == count:
                break
            tops = {e: row(side[e, q], c) for e in range(c + 1, more)}
            scaled = one * inv
            for p in range(q, count):
                if p == q and c + 1 == height:
                    continue
                x = side[c, p] * inv
                panels[p] = panels[p] - x * one
                for e in range(c + 1, more):
                    if (e, p) in side:
                        side[e, p] = side[e, p] - x * tops[e]
        ahead = {c: side[height + c, q + 1] for c in range(height)} if q + 1 < count else {}
        r_ref[base : base + height, :] = jnp.where(lane >= sub + base, out, 0.0)


def factor_kernel(scale, gram_ref, r_ref):
    one, two = gram_ref[0] * scale, gram_ref[1] * scale
    n = one.shape[0]
    size = (S + 1) * n
    b = lambda x, j0, j1: x[:, j0 * n : j1 * n]
    wide = lambda x: jnp.concatenate([x, jnp.zeros((n, size - x.shape[1]), jnp.float32)], axis=1)
    low = jnp.concatenate([
        wide(b(two, 6, 7)),
        wide(b(two, 4, 6)),
        wide(b(two, 1, 4)),
        wide(jnp.concatenate([b(one, 5, 8), b(two, 0, 1)], axis=1)),
        b(one, 0, 5),
    ], axis=0)
    row = lax.broadcasted_iota(jnp.int32, (size, size), 0)
    col = lax.broadcasted_iota(jnp.int32, (size, size), 1)
    a = jnp.where(row >= col, low, low.T)
    height = 8
    cholesky_rows([a[i : i + height] for i in range(0, size, height)], height, r_ref)


def primes(value):
    found, p = [], 2
    while value > 1:
        while value % p == 0:
            found.append(p)
            value //= p
        p += 1
    return found


def sum_stages(chips, grids):
    digits, step = [], 1
    for size in primes(chips):
        digits.append((0, step, size))
        step *= size
    step, places = 1, []
    for size in primes(grids):
        places.append((1, step, size))
        step *= size
    digits[1:1] = places

    def moved(place, digit, by):
        axis, step, size = digit
        now = place[axis] // step % size
        place[axis] += ((now + by) % size - now) * step

    stages = []
    for i in range(0, len(digits), 2):
        pair, group = digits[i : i + 2], []
        for shift in range(1, math.prod(d[2] for d in pair)):
            pairs = []
            for chip in range(chips):
                for core in range(CORES):
                    for grid in range(grids):
                        place = [chip, grid]
                        moved(place, pair[0], shift % pair[0][2])
                        moved(place, pair[-1], shift // pair[0][2])
                        pairs.append(((chip * CORES + core) * grids + grid, (place[0] * CORES + 1 - core) * grids + place[1]))
            group.append(pairs)
        stages.append(group)
    return stages


def local(rhs, blocks, offsets, donor_elem, fringe_elem, donor_weight, fringe_count):
    _, elem_count, n, unknowns = rhs.shape
    chips, cores, grids = (lax.axis_size(a) for a in ("chip", "core", "grid"))
    axes = ("chip", "core", "grid")
    at = lambda chip, core, grid: (chip * cores + core) * grids + grid % grids
    side = []
    for g in range(grids):
        for chip in range(chips - 1):
            side += [(at(chip, 1, g), at(chip + 1, 0, g)), (at(chip + 1, 0, g), at(chip, 1, g))]
        side += [(at(0, 0, g), at(0, 0, g + 1)), (at(chips - 1, 1, g), at(chips - 1, 1, g + 1))]
    swap = [(0, 1), (1, 0)]

    around = [[(g, (g + s) % grids) for g in range(grids)] for s in range(1, grids)]

    def exchange(to_side, to_chip, *to_grids):
        from_side = lax.ppermute(to_side, axes, side)
        others = [lax.ppermute(v, "grid", pairs) for v, pairs in zip(to_grids, around)]
        return from_side, lax.ppermute(to_chip, "core", swap), others

    slots = donor_elem.shape[3]
    halo_type = jax.ShapeDtypeStruct((n, unknowns), jnp.bfloat16)
    side_type = jax.ShapeDtypeStruct((2, n, unknowns), jnp.bfloat16)
    donor_type = jax.ShapeDtypeStruct((slots, n, unknowns), jnp.bfloat16)
    field_type = jax.ShapeDtypeStruct((elem_count, n, unknowns), jnp.bfloat16)
    edge_type = jax.ShapeDtypeStruct((n, unknowns), jnp.float32)
    acc_type = jax.ShapeDtypeStruct((elem_count, n, unknowns), jnp.float32)
    half_type = jax.ShapeDtypeStruct((n, 8 * n), jnp.float32)
    gram_type = jax.ShapeDtypeStruct((2, n, 8 * n), jnp.float32)
    limit = pltpu.CompilerParams(vmem_limit_bytes=24 << 20)
    rhs, blocks = rhs[0], blocks[0]
    flops = 2 * blocks.size * n
    cost = pl.CostEstimate(flops=flops, bytes_accessed=blocks.size * 2, transcendentals=0)
    edge_cost = pl.CostEstimate(flops=flops // elem_count, bytes_accessed=blocks.size * 2 // elem_count, transcendentals=0)

    small = (jnp.transpose(offsets, (2, 0, 1)), donor_elem, fringe_elem, donor_weight, fringe_count)
    messages = exchange(rhs, rhs, *[rhs] * (grids - 1))
    asked = [lax.ppermute(donor_elem, "grid", pairs) for pairs in around]
    offset, *small = pl.pallas_call(
        start_kernel,
        out_shape=tuple(pltpu.SMEM(x.shape, x.dtype) for x in small),
        in_specs=[HBM] * 5, out_specs=(SMEM,) * 5,
        scratch_shapes=[pltpu.SemaphoreType.DMA((5,))],
        compiler_params=limit, name="start",
        cost_estimate=pl.CostEstimate(flops=2 * 10**9, bytes_accessed=10**6, transcendentals=0),
    )(*(pltpu.with_memory_space_constraint(x, pltpu.HBM) for x in small))
    field = rhs
    basis = [field]
    for level in range(S):
        from_side, from_chip, others = messages
        acc = pl.pallas_call(
            inner_kernel, out_shape=acc_type, in_specs=[SMEM, VMEM, VMEM], out_specs=VMEM,
            compiler_params=limit, name="inner", cost_estimate=cost,
        )(offset, field, blocks)
        edge = lambda in_chip, halo: pl.pallas_call(
            functools.partial(edge_kernel, in_chip), out_shape=edge_type, in_specs=[SMEM, VMEM, VMEM], out_specs=VMEM,
            compiler_params=limit, name="chip_edge" if in_chip else "side_edge", cost_estimate=edge_cost,
        )(offset, halo, blocks)
        shared = (*small, acc, edge(True, from_chip))
        side_in = (offset, from_side, blocks) if level == 0 else (edge(False, from_side),)
        if level + 1 < S:
            field, *sends = pl.pallas_call(
                functools.partial(outer_kernel, grids, level == 0),
                out_shape=(field_type, side_type, halo_type, *[donor_type] * (grids - 1)),
                in_specs=[SMEM] * 4 + [VMEM] * (2 + 2 * (grids - 1)) + ([SMEM] if level == 0 else []) + [VMEM] * len(side_in[-2:]),
                out_specs=(VMEM,) * (3 + grids - 1),
                scratch_shapes=[pltpu.VMEM((n, unknowns), jnp.float32)] if level == 0 else [],
                compiler_params=limit, name="outer",
            )(*shared, *asked, *others, *side_in)
            messages = exchange(*sends)
        else:
            early = pl.pallas_call(
                early_gram_kernel, out_shape=(half_type, half_type),
                in_specs=[VMEM] * S, out_specs=(VMEM, VMEM), compiler_params=limit, name="early_gram", cost_estimate=cost,
            )(*basis)
            field, gram = pl.pallas_call(
                functools.partial(last_kernel, grids), out_shape=(field_type, gram_type),
                in_specs=[SMEM] * 4 + [VMEM] * (3 + grids - 1 + S + 2), out_specs=(VMEM,) * 2,
                compiler_params=limit, name="last",
            )(*shared, *others, *side_in, *basis, *early)
        basis.append(field)
    gram = gram + lax.ppermute(gram, "core", swap)
    for group in sum_stages(chips, grids):
        arrived = [lax.ppermute(gram, axes, pairs) for pairs in group]
        for part in arrived:
            gram = gram + part
    columns = (S + 1) * n
    row_total = grids * chips * cores * elem_count * unknowns
    r_factor = pl.pallas_call(
        functools.partial(factor_kernel, 1.0 / row_total),
        out_shape=jax.ShapeDtypeStruct((columns, columns), jnp.float32),
        in_specs=[VMEM], out_specs=VMEM,
        compiler_params=limit, name="factor",
    )(gram)
    powers = jnp.stack(basis[1:], axis=1)[None]
    return (powers, r_factor)


def solution(mesh):
    dom, grids = mesh.shape["dom"], mesh.shape["grid"]
    split = Mesh(mesh.devices.reshape(dom // CORES, CORES, grids), ("chip", "core", "grid"))
    where = ("chip", "core")
    in_specs = (
        P("grid", where, None, None),
        P("grid", where, None, None, None),
        P("grid", where, None),
        P("grid", where, None, None),
        P("grid", where, None, None),
        P("grid", where, None, None),
        P("grid", where, None),
    )
    out_specs = (P("grid", where, None, None, None), P())
    return jax.shard_map(local, mesh=split, in_specs=in_specs, out_specs=out_specs, check_vma=False)
```
